256 devices in a mesh: term: 8 (over x, core), sector: 32 (over y, z).
Axes of the slice: x: 4, y: 4, z: 8, core: 2. Of those that a mesh axis runs over, the one named last changes fastest.
Arguments:
- psi: bfloat16 [256, 256, 256], P('sector'), may hold values from -6 to 6
- left_env: bfloat16 [8, 128, 4, 256, 256], P('term', 'sector'), may hold values from -0.375 to 0.375
- right_env: bfloat16 [8, 128, 4, 256, 256], P('term', 'sector'), may hold values from -0.375 to 0.375
- pair_source: int32 [1024], P('sector'), may hold values from 0 to 7
- pair_left: int32 [1024], P('sector'), may hold values from 0 to 3
- pair_right: int32 [1024], P('sector'), may hold values from 0 to 3
- pair_dest: int32 [1024, 1], P('sector'), may hold values from 0 to 31; in each aligned block of 32 rows (0 to 31, 32 to 63, ...) at most 2 rows name the same one
- pair_target: int32 [1024], P('sector'), may hold values from 0 to 7
Outputs:
- sigma: bfloat16 [256, 256, 256], P('sector', 'term')
The draws below stay inside these ranges and needn't reach their ends.
Inputs may be any that keep to these rules, and one draw needn't show every extreme that they name: `pair_dest`: among the 32 pairs of one sector index, at most 2 name the same owner, a bound that some block reaches.
All inputs are finite; a program needn't handle non-finite values.
Results may differ from the reference program's by a relative error of at most 0.014.
Values may be sent and summed in bfloat16 or wider, within the bound.
A program may use at most 128 MiB of HBM per device.

```python
import math
import jax
import jax.numpy as jnp
import numpy as np
from jax import lax

BLK = 256
TERMS = 4
SEC_DEV = 8
PAIRS = 32
ENV_DEV = 4
CAP = 2
TERM_GROUPS = 8
SECTORS = 256
ENVS = 128
PAIRS_ALL = 1024
N_SECTOR = 32


def place_ends(array, key, least, high):
    longest = array.shape.index(max(array.shape))
    spots = []
    for shift in (0, 1):
        where = [jax.random.randint(jax.random.fold_in(key, axis), (), 0, length) for axis, length in enumerate(array.shape)]
        where[longest] = (where[longest] + shift) % array.shape[longest]
        spots.append(tuple(where))
    return array.at[spots[0]].set(least).at[spots[1]].set(high)


def block_scale(key, shape, pieces, low, top_value):
    def one(dim, parts):
        steps = jax.random.uniform(jax.random.fold_in(jax.random.fold_in(key, 6), dim), (parts,), jnp.float32, low / len(pieces), top_value / len(pieces))
        return jnp.repeat(jnp.exp(steps), shape[dim] // parts).reshape((-1,) + (1,) * (len(shape) - dim - 1))

    factor_of = one(*pieces[0])
    for cut in pieces[1:]:
        factor_of = factor_of * one(*cut)
    return factor_of


def deal_out(key, own, number, rows, count, top, bound, skew):
    sequence = jax.random.permutation(key, count)
    packed, usual = shares(count, rows * top, bound, skew, True), shares(count, rows * top, bound, skew, False)
    places = jnp.arange(count)

    def named(lengths, turn):
        used = int((lengths > 0).sum())
        fixed = max(1, used // 4)
        passed = fixed + (places - fixed + turn * (used - fixed)) % max(1, count - fixed)
        return jnp.zeros((count,), jnp.int32).at[sequence[jnp.where(places < fixed, places, passed)]].set(jnp.asarray(lengths, jnp.int32))

    lengths = jnp.where(number % 4 == 0, named(packed, number // 4), named(usual, number - number // 4 - 1))
    mixed = jax.random.permutation(jax.random.fold_in(own, 3), count)
    giver, sink = mixed[0:count // 2 * 2:2], mixed[1:count // 2 * 2:2]
    margin = jnp.minimum(lengths[giver] - 1, bound - lengths[sink]) // 2
    margin = jnp.where((giver == sequence[0]) | (sink == sequence[0]) | (lengths[sink] == 0), 0, jnp.maximum(margin, 0))
    passed = jax.random.randint(jax.random.fold_in(own, 4), (count // 2,), 0, 1 << 20) % (margin + 1)
    lengths = lengths.at[giver].add(-passed).at[sink].add(passed)
    members = jnp.searchsorted(jnp.cumsum(lengths), jnp.arange(rows * top), side="right").astype(jnp.int32)
    grid = members.reshape(top, rows).T
    grid = grid[jax.random.permutation(jax.random.fold_in(own, 1), rows)]
    turn = jax.random.randint(jax.random.fold_in(own, 2), (rows, 1), 0, top)
    return jnp.take_along_axis(grid, (jnp.arange(top)[None, :] + turn) % top, axis=1)


def shares(count, total, most, skew, full):
    loads = [(1 << 20) // math.isqrt(grade ** skew) + 1 for grade in range(1, count + 1)]
    largest = most if full else min(most, max(-(-total // count), total * loads[0] // sum(loads)))
    least = 1 if total - largest >= count - 1 else 0
    counts, surplus = [largest] + [least] * (count - 1), total - largest - least * (count - 1)
    while surplus > 0:
        free = [i for i in range(1, count) if counts[i] < largest] or [i for i in range(1, count) if counts[i] < most]
        mass, left = sum([loads[i] for i in free]), surplus
        for i in free:
            more = min(most - counts[i], max(1, left * loads[i] // mass), surplus)
            counts[i] = counts[i] + more
            surplus = surplus - more
    return np.array(counts)


def bell_draw(rng, dims, deviation, limit, cuts=(), held_as=jnp.bfloat16):
    gain = block_scale(rng, dims, cuts, -0.22, 0.18) if cuts else 1.0
    result = jax.random.normal(rng, dims, jnp.float32) * deviation * gain
    return jnp.minimum(jnp.maximum(result, -limit), limit).astype(held_as)


def setup_inputs(seed: int = 0) -> dict:
    keys = jax.random.split(jax.random.key(seed), 9)
    psi = bell_draw(keys[0], (SECTORS, BLK, BLK), 1.0, 6.0, ((0, 32),))
    left_env = bell_draw(keys[1], (TERM_GROUPS, ENVS, TERMS, BLK, BLK), BLK ** -0.5, 0.375, ((0, 8), (1, 32)))
    right_env = bell_draw(keys[2], (TERM_GROUPS, ENVS, TERMS, BLK, BLK), BLK ** -0.5, 0.375, ((0, 8), (1, 32)))
    pair_source = place_ends(jax.random.randint(keys[3], (PAIRS_ALL,), 0, SEC_DEV), jax.random.fold_in(keys[3], 1), 0, SEC_DEV - 1).astype(jnp.int32)
    pair_left = place_ends(jax.random.randint(keys[4], (PAIRS_ALL,), 0, ENV_DEV), jax.random.fold_in(keys[4], 1), 0, ENV_DEV - 1).astype(jnp.int32)
    pair_right = place_ends(jax.random.randint(keys[5], (PAIRS_ALL,), 0, ENV_DEV), jax.random.fold_in(keys[5], 1), 0, ENV_DEV - 1).astype(jnp.int32)
    pair_dest_keys = jax.random.split(jax.random.fold_in(keys[6], 1), PAIRS_ALL // PAIRS)
    pair_dest_turns = jax.random.permutation(jax.random.fold_in(keys[6], 3), PAIRS_ALL // PAIRS)
    pair_dest = jax.vmap(lambda own, number: deal_out(jax.random.fold_in(keys[6], 2), own, number, PAIRS, N_SECTOR, 1, CAP, 2))(pair_dest_keys, pair_dest_turns).reshape((PAIRS_ALL, 1))
    pair_target = place_ends(jax.random.randint(keys[7], (PAIRS_ALL,), 0, SEC_DEV), jax.random.fold_in(keys[7], 1), 0, SEC_DEV - 1).astype(jnp.int32)
    return dict(psi=psi, left_env=left_env, right_env=right_env, pair_source=pair_source, pair_left=pair_left, pair_right=pair_right, pair_dest=pair_dest, pair_target=pair_target)


def reference(psi, left_env, right_env, pair_source, pair_left, pair_right, pair_dest, pair_target):
    shard_of = (jnp.arange(PAIRS_ALL, dtype=jnp.int32) // PAIRS).astype(jnp.int32)
    source_all = shard_of * SEC_DEV + pair_source
    left_all = shard_of * ENV_DEV + pair_left
    right_all = shard_of * ENV_DEV + pair_right
    target_all = pair_dest[:, 0] * SEC_DEV + pair_target
    source_blocks = source_all.reshape(N_SECTOR, PAIRS)
    left_blocks = left_all.reshape(N_SECTOR, PAIRS)
    right_blocks = right_all.reshape(N_SECTOR, PAIRS)
    target_blocks = target_all.reshape(N_SECTOR, PAIRS)

    def one_group(carry, group):
        left_group = left_env[group]
        right_group = right_env[group]

        def one_shard(total, idx):
            src, lft, rgt, tgt = idx
            source_here = psi[src].astype(jnp.float32)
            accum = jnp.zeros((PAIRS, BLK, BLK), jnp.float32)
            for mpo_term in range(TERMS):
                inner = jnp.einsum("pij,pjk->pik", source_here, right_group[rgt, mpo_term].astype(jnp.float32)).astype(jnp.bfloat16)
                accum = accum + jnp.einsum("pij,pjk->pik", left_group[lft, mpo_term].astype(jnp.float32), inner.astype(jnp.float32))
            part = accum.astype(jnp.bfloat16)
            return total.at[tgt].add(part.astype(jnp.float32)), None

        carry, _ = lax.scan(one_shard, carry, (source_blocks, left_blocks, right_blocks, target_blocks))
        return carry, None

    start = jnp.zeros((SECTORS, BLK, BLK), jnp.float32)
    total, _ = lax.scan(one_group, start, jnp.arange(TERM_GROUPS, dtype=jnp.int32))
    return total.astype(jnp.bfloat16)
```

```python
import jax
import jax.numpy as jnp
from jax import lax
from jax.sharding import PartitionSpec as P


def shards(psi, left_env, right_env, pair_source, pair_left, pair_right, pair_dest, pair_target):
    owners = lax.axis_size("sector")
    owned = psi.shape[0]
    width = psi.shape[1]
    count = pair_source.shape[0]
    slots_each = max(2, 2 * count // owners)
    slots = owners * slots_each
    left_local = left_env[0]
    right_local = right_env[0]
    terms_here = left_local.shape[1]
    source_blocks = psi[pair_source]
    accum = jnp.zeros((count, width, width), jnp.float32)
    for mpo_term in range(terms_here):
        inner = jnp.einsum(
            "pij,pjk->pik",
            source_blocks,
            right_local[pair_right, mpo_term],
            preferred_element_type=jnp.float32,
        ).astype(jnp.bfloat16)
        accum = accum + jnp.einsum(
            "pij,pjk->pik",
            left_local[pair_left, mpo_term],
            inner,
            preferred_element_type=jnp.float32,
        )
    part = accum.astype(jnp.bfloat16)
    mine = lax.psum_scatter(part, "term", scatter_dimension=1, tiled=True)
    rows = mine.shape[1]
    owner_of = pair_dest[:, 0]
    onehot = (owner_of[:, None] == jnp.arange(owners, dtype=jnp.int32)[None, :]).astype(jnp.int32)
    earlier = jnp.cumsum(onehot, axis=0) - onehot
    slot_of = jnp.sum(earlier * onehot, axis=1)
    position = owner_of * slots_each + slot_of
    labels = jnp.full((slots,), -1, jnp.int32).at[position].set(pair_target)
    outgoing = jnp.zeros((slots, rows, width), jnp.bfloat16).at[position].set(mine)
    arrived, arrived_labels = (
        lax.all_to_all(outgoing, "sector", split_axis=0, concat_axis=0, tiled=True),
        lax.all_to_all(labels, "sector", split_axis=0, concat_axis=0, tiled=True),
    )
    select = (arrived_labels[None, :] == jnp.arange(owned, dtype=jnp.int32)[:, None]).astype(
        jnp.bfloat16
    )
    gathered = jnp.dot(
        select, arrived.reshape(slots, rows * width), preferred_element_type=jnp.float32
    )
    return gathered.reshape(owned, rows, width).astype(jnp.bfloat16)


def solution(mesh):
    placed = (
        P("sector", None, None),
        P("term", "sector", None, None, None),
        P("term", "sector", None, None, None),
        P("sector"),
        P("sector"),
        P("sector"),
        P("sector", None),
        P("sector"),
    )
    return jax.shard_map(
        shards, mesh=mesh, in_specs=placed, out_specs=P("sector", "term", None), check_vma=False
    )
```

```python
import jax
import jax.numpy as jnp
from jax import lax
from jax.experimental import pallas as pl
from jax.experimental.pallas import tpu as pltpu
from jax.sharding import PartitionSpec as P

MESH = pl.DeviceIdType.MESH
F32, BF16, I32 = jnp.float32, jnp.bfloat16, jnp.int32

NX, NCORE, NY, NZ = 4, 2, 4, 8
PAIRS, TERMS, OWNED, WIDTH = 32, 4, 8, 256
ROWS = 16
BATCH = 4
NB = PAIRS // BATCH
LEFT, RIGHT = 0, 1


def kernel(
    psi_hbm, left_hbm, right_hbm, src_hbm, lft_hbm, rgt_hbm, dest_hbm, tgt_hbm,
    out_ref,
    psi, lenv, renv, src_s, lft_s, rgt_s, dest_s, tgt_s,
    inner, part, core_in, a_out, a_in, b_out, b_in, y0, y1, dens, z_out, z_in,
    dcol, tcol, meta, meta_s,
    load_sem, meta_sem, meta_send, meta_recv,
    core_send, core_recv, a_send, a_recv, b_send, b_recv,
    y1_send, y1_recv, y2_send, y2_recv, z_send, z_recv,
):
    term, sector = lax.axis_index("term"), lax.axis_index("sector")
    x, c = term // NCORE, term % NCORE
    y, z = sector // NZ, sector % NZ
    yv = (y0, y1)

    def at_x(d):
        return (((x + d) % NX) * NCORE + c, sector)

    def at_y(d):
        return (term, ((y + d) % NY) * NZ + z)

    def at_z(d):
        return (term, y * NZ + (z + d) % NZ)

    partner = (x * NCORE + 1 - c, sector)
    x_dev = (at_x(NX - 1), at_x(1))
    y_dev = (at_y(NY - 1), at_y(1))
    z_dev = (at_z(NZ - 1), at_z(1))

    small = [(src_hbm, src_s), (lft_hbm, lft_s), (rgt_hbm, rgt_s), (dest_hbm, dest_s), (tgt_hbm, tgt_s)]
    loads = small + [(psi_hbm, psi), (right_hbm, renv), (left_hbm, lenv)]
    loads = [pltpu.make_async_copy(a, b, load_sem.at[i]) for i, (a, b) in enumerate(loads)]
    for cp in loads:
        cp.start()

    barrier = pltpu.get_barrier_semaphore()
    peers = (partner,) + x_dev + y_dev + (at_y(2),) + z_dev
    for dev in peers:
        pl.semaphore_signal(barrier, inc=1, device_id=dev, device_id_type=MESH)

    def remote(src, dst, send, recv, dev):
        return pltpu.make_async_remote_copy(
            src_ref=src, dst_ref=dst, send_sem=send, recv_sem=recv, device_id=dev, device_id_type=MESH
        )

    def first(b):
        for j in range(BATCH):
            p = b * BATCH + j
            rows = psi[src_s[p]]
            r = rgt_s[p]
            for k in range(TERMS):
                inner[p, k] = jnp.dot(rows, renv[r, k], preferred_element_type=F32).astype(BF16)

    def second(h, b):
        t = h * NB + b
        for j in range(BATCH):
            p = b * BATCH + j
            l = lft_s[p]
            acc = None
            for k in range(TERMS):
                lhs = lenv[l, k, :, h].reshape(NX * NCORE * ROWS, WIDTH)
                d = jnp.dot(lhs, inner[p, k], preferred_element_type=F32)
                acc = d if acc is None else acc + d
            for xx in range(NX):
                for cc in range(NCORE):
                    r = (xx * NCORE + cc) * ROWS
                    part[cc, t, xx, j] = acc[r : r + ROWS].astype(BF16)

    def core_copy(t):
        return remote(part.at[1 - c, t], core_in.at[t], core_send.at[t], core_recv.at[t], partner)

    def a_copy(t, d):
        return remote(a_out.at[t, d], a_in.at[t, d], a_send.at[t, d], a_recv.at[t, d], x_dev[d])

    def b_copy(t, d):
        return remote(b_out.at[t, d], b_in.at[t, d], b_send.at[t, d], b_recv.at[t, d], x_dev[d])

    def y1_copy(h, b, d):
        t = h * NB + b
        ps = pl.ds(b * BATCH, BATCH)
        return remote(yv[h].at[0, ps], yv[h].at[3 if d == LEFT else 1, ps], y1_send.at[t, d], y1_recv.at[t, d], y_dev[d])

    def y2_copy(h, b, d):
        t = h * NB + b
        ps = pl.ds(b * BATCH + (BATCH // 2 if d == LEFT else 0), BATCH // 2)
        return remote(
            yv[h].at[3 if d == LEFT else 1, ps], yv[h].at[2, ps], y2_send.at[t, d], y2_recv.at[t, d], y_dev[d]
        )

    def chip_sum(t, d, lo, hi):
        xx = (x + d) % NX
        return part[c, t, xx, lo:hi].astype(F32) + core_in[t, xx, lo:hi].astype(F32)

    half = BATCH // 2

    def stage1(t):
        core_copy(t).wait_recv()
        a_out[t, LEFT] = chip_sum(t, 2, 0, half).astype(BF16)
        a_out[t, RIGHT] = chip_sum(t, 2, half, BATCH).astype(BF16)
        a_copy(t, LEFT).start()
        a_copy(t, RIGHT).start()

    def stage2(t):
        a_copy(t, LEFT).wait_recv()
        a_copy(t, RIGHT).wait_recv()
        b_out[t, LEFT, :half] = (chip_sum(t, 3, 0, half) + a_in[t, LEFT].astype(F32)).astype(BF16)
        b_out[t, LEFT, half:] = chip_sum(t, 3, half, BATCH).astype(BF16)
        b_out[t, RIGHT, :half] = chip_sum(t, 1, 0, half).astype(BF16)
        b_out[t, RIGHT, half:] = (chip_sum(t, 1, half, BATCH) + a_in[t, RIGHT].astype(F32)).astype(BF16)
        b_copy(t, LEFT).start()
        b_copy(t, RIGHT).start()

    def stage3(h, b):
        t = h * NB + b
        b_copy(t, LEFT).wait_recv()
        b_copy(t, RIGHT).wait_recv()
        total = chip_sum(t, 0, 0, BATCH) + b_in[t, LEFT].astype(F32) + b_in[t, RIGHT].astype(F32)
        yv[h][0, pl.ds(b * BATCH, BATCH)] = total.astype(BF16)
        y1_copy(h, b, LEFT).start()
        y1_copy(h, b, RIGHT).start()

    def stage4(h, b):
        y1_copy(h, b, LEFT).wait_recv()
        y1_copy(h, b, RIGHT).wait_recv()
        y2_copy(h, b, LEFT).start()
        y2_copy(h, b, RIGHT).start()

    def y2_wait(h):
        def body(b, _):
            y2_copy(h, b, LEFT).wait_recv()
            y2_copy(h, b, RIGHT).wait_recv()
            return 0

        lax.fori_loop(0, NB, body, 0)

    def densify(h, dz, slot):
        o = y * NZ + (z + dz) % NZ
        blocks, labels = [], []
        for r in range(NY):
            for q in range(2):
                blocks.append(yv[h][r, meta_s[r, q, o]].astype(F32))
                labels.append(meta_s[r, 2 + q, o])
        for t in range(OWNED):
            acc = None
            for blk, lab in zip(blocks, labels):
                term_ = blk * jnp.where(lab == t, 1.0, 0.0).astype(F32)
                acc = term_ if acc is None else acc + term_
            dens[slot, t] = acc

    HALF_T = OWNED // 2

    def z_copy(h, hop, d):
        ts = pl.ds(0, OWNED) if hop else pl.ds(HALF_T if d == LEFT else 0, HALF_T)
        return remote(
            z_out.at[h, hop, d, ts], z_in.at[h, hop, d, ts], z_send.at[h, hop, d], z_recv.at[h, hop, d], z_dev[d]
        )

    def z_step(h, hop):
        if hop == 0:
            densify(h, 4, 0)
            for d in (LEFT, RIGHT):
                ts = slice(HALF_T, OWNED) if d == LEFT else slice(0, HALF_T)
                z_out[h, 0, d, ts] = dens[0, ts].astype(BF16)
                z_copy(h, 0, d).start()
        elif hop < 4:
            densify(h, (4 + hop) % NZ, LEFT)
            densify(h, 4 - hop, RIGHT)
            for d in (LEFT, RIGHT):
                z_copy(h, hop - 1, d).wait_recv()
                if hop == 1:
                    ts = slice(HALF_T, OWNED) if d == LEFT else slice(0, HALF_T)
                    no = slice(0, HALF_T) if d == LEFT else slice(HALF_T, OWNED)
                    z_out[h, 1, d, ts] = (dens[d, ts] + z_in[h, 0, d, ts].astype(F32)).astype(BF16)
                    z_out[h, 1, d, no] = dens[d, no].astype(BF16)
                else:
                    z_out[h, hop, d] = (dens[d] + z_in[h, hop - 1, d].astype(F32)).astype(BF16)
                z_copy(h, hop, d).start()
        else:
            densify(h, 0, 0)
            z_copy(h, 3, LEFT).wait_recv()
            z_copy(h, 3, RIGHT).wait_recv()
            total = dens[0] + z_in[h, 3, LEFT].astype(F32) + z_in[h, 3, RIGHT].astype(F32)
            out_ref[:, h * ROWS : (h + 1) * ROWS, :] = total.astype(BF16)

    for cp in loads[:7]:
        cp.wait()
    for p in range(PAIRS):
        dcol[p] = jnp.full((128,), dest_s[p], I32)
        tcol[p] = jnp.full((128,), tgt_s[p], I32)
    lane = lax.broadcasted_iota(I32, (PAIRS, 128), 1)
    prow = lax.broadcasted_iota(I32, (PAIRS, 128), 0)
    same = dcol[...] == lane
    low = jnp.min(jnp.where(same, prow, PAIRS), axis=0, keepdims=True)
    high = jnp.max(jnp.where(same, prow, -1), axis=0, keepdims=True)
    low_t = jnp.max(jnp.where(same & (prow == low), tcol[...], -1), axis=0, keepdims=True)
    high_t = jnp.max(jnp.where(same & (prow == high) & (high > low), tcol[...], -1), axis=0, keepdims=True)
    meta[0] = jnp.zeros((8, 128), I32)
    meta[0, 0:1] = jnp.clip(low, 0, PAIRS - 1)
    meta[0, 1:2] = jnp.clip(high, 0, PAIRS - 1)
    meta[0, 2:3] = low_t
    meta[0, 3:4] = high_t

    first(0)
    loads[7].wait()
    pl.semaphore_wait(barrier, len(peers))

    def meta_copy(r):
        return remote(meta.at[0], meta.at[r], meta_send.at[r], meta_recv.at[r], at_y(r))

    for r in range(1, NY):
        meta_copy(r).start()

    def loop0(b, _):
        second(0, b)
        core_copy(b).start()
        first(b + 1)

        @pl.when(b >= 1)
        def _():
            stage1(b - 1)

        @pl.when(b >= 2)
        def _():
            stage2(b - 2)

        @pl.when(b >= 3)
        def _():
            stage3(0, b - 3)

        @pl.when(b >= 4)
        def _():
            stage4(0, b - 4)

        return 0

    lax.fori_loop(0, NB - 1, loop0, 0)
    second(0, NB - 1)
    core_copy(NB - 1).start()
    stage1(NB - 2)
    stage2(NB - 3)
    stage3(0, NB - 4)
    stage4(0, NB - 5)

    for r in range(1, NY):
        meta_copy(r).wait_recv()
    to_smem = pltpu.make_async_copy(meta, meta_s, meta_sem)
    to_smem.start()
    to_smem.wait()

    def both(b, lag, stage):
        @pl.when(b < lag)
        def _():
            stage(0, b + NB - lag)

        @pl.when(b >= lag)
        def _():
            stage(1, b - lag)

    def loop1(b, _):
        second(1, b)
        core_copy(NB + b).start()
        stage1(NB + b - 1)
        stage2(NB + b - 2)
        both(b, 3, stage3)
        both(b, 4, stage4)

        @pl.when(b == 5)
        def _():
            y2_wait(0)
            z_step(0, 0)

        @pl.when(b == 7)
        def _():
            z_step(0, 1)

        return 0

    lax.fori_loop(0, NB, loop1, 0)
    stage1(2 * NB - 1)
    stage2(2 * NB - 2)
    stage3(1, NB - 3)
    stage4(1, NB - 4)
    stage2(2 * NB - 1)
    stage3(1, NB - 2)
    stage4(1, NB - 3)
    z_step(0, 2)
    stage3(1, NB - 1)
    stage4(1, NB - 2)
    z_step(0, 3)
    stage4(1, NB - 1)
    z_step(0, 4)
    y2_wait(1)
    for hop in range(5):
        z_step(1, hop)

    for r in range(1, NY):
        meta_copy(r).wait_send()

    def sent(b, _):
        for h in range(2):
            t = h * NB + b
            core_copy(t).wait_send()
            for d in (LEFT, RIGHT):
                a_copy(t, d).wait_send()
                b_copy(t, d).wait_send()
                y1_copy(h, b, d).wait_send()
                y2_copy(h, b, d).wait_send()
        return 0

    lax.fori_loop(0, NB, sent, 0)
    for h in range(2):
        for hop in range(4):
            for d in (LEFT, RIGHT):
                z_copy(h, hop, d).wait_send()


def shards(psi, left_env, right_env, pair_source, pair_left, pair_right, pair_dest, pair_target):
    steps = 2 * NB
    block = (ROWS, WIDTH)
    dma = pltpu.SemaphoreType.DMA
    return pl.pallas_call(
        kernel,
        out_shape=jax.ShapeDtypeStruct((OWNED, 2 * ROWS, WIDTH), BF16),
        in_specs=[pl.BlockSpec(memory_space=pl.ANY)] * 8,
        out_specs=pl.BlockSpec(memory_space=pltpu.VMEM),
        scratch_shapes=[
            pltpu.VMEM((OWNED, WIDTH, WIDTH), BF16),
            pltpu.VMEM((4, TERMS, NX * NCORE, 2) + block, BF16),
            pltpu.VMEM((4, TERMS, WIDTH, WIDTH), BF16),
        ]
        + [pltpu.SMEM((PAIRS,), I32)] * 5
        + [
            pltpu.VMEM((PAIRS, TERMS, WIDTH, WIDTH), BF16),
            pltpu.VMEM((NCORE, steps, NX, BATCH) + block, BF16),
            pltpu.VMEM((steps, NX, BATCH) + block, BF16),
            pltpu.VMEM((steps, 2, BATCH // 2) + block, BF16),
            pltpu.VMEM((steps, 2, BATCH // 2) + block, BF16),
            pltpu.VMEM((steps, 2, BATCH) + block, BF16),
            pltpu.VMEM((steps, 2, BATCH) + block, BF16),
            pltpu.VMEM((NY, PAIRS) + block, BF16),
            pltpu.VMEM((NY, PAIRS) + block, BF16),
            pltpu.VMEM((2, OWNED) + block, F32),
            pltpu.VMEM((2, 4, 2, OWNED) + block, BF16),
            pltpu.VMEM((2, 4, 2, OWNED) + block, BF16),
            pltpu.VMEM((PAIRS, 128), I32),
            pltpu.VMEM((PAIRS, 128), I32),
            pltpu.VMEM((NY, 8, 128), I32),
            pltpu.SMEM((NY, 8, 128), I32),
            dma((8,)), dma, dma((NY,)), dma((NY,)),
            dma((steps,)), dma((steps,)),
            dma((steps, 2)), dma((steps, 2)), dma((steps, 2)), dma((steps, 2)),
            dma((steps, 2)), dma((steps, 2)), dma((steps, 2)), dma((steps, 2)),
            dma((2, 4, 2)), dma((2, 4, 2)),
        ],
        compiler_params=pltpu.CompilerParams(
            collective_id=0, has_side_effects=True, vmem_limit_bytes=56 * 2**20
        ),
        name="sigma",
    )(
        psi,
        left_env.reshape((4, TERMS, NX * NCORE, 2) + block),
        right_env.reshape((4, TERMS, WIDTH, WIDTH)),
        pair_source, pair_left, pair_right, pair_dest.reshape(PAIRS), pair_target,
    )


def solution(mesh):
    placed = (
        P("sector", None, None),
        P("term", "sector", None, None, None),
        P("term", "sector", None, None, None),
        P("sector"),
        P("sector"),
        P("sector"),
        P("sector", None),
        P("sector"),
    )
    return jax.shard_map(
        shards, mesh=mesh, in_specs=placed, out_specs=P("sector", "term", None), check_vma=False
    )
```

```python
import jax
import jax.numpy as jnp
from jax import lax
from jax.experimental import pallas as pl
from jax.experimental.pallas import tpu as pltpu
from jax.sharding import PartitionSpec as P

MESH = pl.DeviceIdType.MESH
F32, BF16, I32 = jnp.float32, jnp.bfloat16, jnp.int32

NX, NCORE, NY, NZ = 4, 2, 4, 8
NS = NY * NZ
PAIRS, TERMS, OWNED, WIDTH = 32, 4, 8, 256
ROWS = 16
BATCH = 8
NB = PAIRS // BATCH
CAP = 2
GROUPS = ((16, 32), (1, 16))
GROUP = [1] * 16 + [0] * 16
ORDER = [d for lo, hi in GROUPS for d in sorted(range(lo, hi), key=lambda d: abs(d % NZ - NZ // 2))] + [0]


def kernel(
    psi_hbm, left_hbm, right_hbm, src_hbm, lft_hbm, rgt_hbm, dest_hbm, tgt_hbm,
    out_ref,
    psi, lenv, renv, src_s, lft_s, rgt_s, dest_s, tgt_s,
    inner, part, core_in, x_out, x_in, red, slot_out, slot_in,
    dcol, tcol, table_s, tables, labels,
    load_sem, table_sem, ty_send, ty_recv, tz_send, tz_recv,
    core_send, core_recv, x_send, x_recv, s_send, s_recv,
):
    term, sector = lax.axis_index("term"), lax.axis_index("sector")
    x, c = term // NCORE, term % NCORE
    y, z = sector // NZ, sector % NZ

    x_at = [lax.rem(x + d, NX) for d in range(NX)]
    y_at = [lax.rem(y + d, NY) * NZ for d in range(NY)]
    z_at = [lax.rem(z + d, NZ) for d in range(NZ)]

    def at_x(d):
        return (x_at[d] * NCORE + c, sector)

    def owner(d):
        return y_at[d // NZ] + z_at[d % NZ]

    def at_s(d):
        return (term, owner(d))

    partner = (x * NCORE + 1 - c, sector)

    small = [(src_hbm, src_s), (lft_hbm, lft_s), (rgt_hbm, rgt_s), (dest_hbm, dest_s), (tgt_hbm, tgt_s)]
    loads = small + [(psi_hbm, psi), (right_hbm, renv), (left_hbm, lenv)]
    loads = [pltpu.make_async_copy(a, b, load_sem.at[i]) for i, (a, b) in enumerate(loads)]
    for cp in loads:
        cp.start()

    barrier = pltpu.get_barrier_semaphore()

    def greet(dev):
        pl.semaphore_signal(barrier, inc=1, device_id=dev, device_id_type=MESH)

    greet(partner)
    for d in range(1, NX):
        greet(at_x(d))

    for d in range(1, NS):
        greet(at_s(d))

    def remote(src, dst, send, recv, dev):
        return pltpu.make_async_remote_copy(
            src_ref=src, dst_ref=dst, send_sem=send, recv_sem=recv, device_id=dev, device_id_type=MESH
        )

    def compute(b):
        for k in range(TERMS):
            for j in range(BATCH):
                p = b * BATCH + j
                inner[j, k] = jnp.dot(psi[src_s[p]], renv[rgt_s[p], k], preferred_element_type=F32).astype(BF16)
        for j in range(BATCH):
            l = lft_s[b * BATCH + j]
            acc = None
            for k in range(TERMS):
                d = jnp.dot(lenv[l, k], inner[j, k], preferred_element_type=F32)
                acc = d if acc is None else acc + d
            for xx in range(NX):
                for cc in range(NCORE):
                    for h in range(2):
                        r = ((xx * NCORE + cc) * 2 + h) * ROWS
                        part[h, cc, b, xx, j] = acc[r : r + ROWS].astype(BF16)

    def core_copy(h, b):
        return remote(part.at[h, 1 - c, b], core_in.at[h, b], core_send.at[h], core_recv.at[h, b], partner)

    def x_copy(h, b, d):
        return remote(x_out.at[h, b, d - 1], x_in.at[h, b, d - 1], x_send.at[h], x_recv.at[h, b], at_x(d))

    def chip_sum(h, b, d):
        xx = x_at[d]
        return part[h, c, b, xx].astype(F32) + core_in[h, b, xx].astype(F32)

    def stage_x(h, b):
        core_copy(h, b).wait_recv()
        for d in (2, 1, 3):
            x_out[h, b, d - 1] = chip_sum(h, b, d).astype(BF16)
            x_copy(h, b, d).start()

    def stage_sum(h, b):
        remote(x_out.at[h, b], x_in.at[h, b], x_send.at[h], x_recv.at[h, b], at_x(1)).wait_recv()
        total = chip_sum(h, b, 0)
        for d in (1, 2, 3):
            total = total + x_in[h, b, d - 1].astype(F32)
        red[h, pl.ds(b * BATCH, BATCH)] = total.astype(BF16)

    def s_copy(h, d):
        return remote(slot_out.at[h, d], slot_in.at[h, d], s_send.at[h], s_recv.at[h, GROUP[d]], at_s(d))

    def send_slots(h):
        for d in ORDER:
            o = owner(d)
            for q in range(CAP):
                (slot_out if d else slot_in)[h, d, q] = red[h, table_s[q, o]]
            if d:
                s_copy(h, d).start()

    def finish(h):
        acc = [jnp.zeros((ROWS, WIDTH), F32) for _ in range(OWNED)]
        for g, (lo, hi) in enumerate(GROUPS):
            remote(
                slot_out.at[h, lo:hi], slot_in.at[h, lo:hi], s_send.at[h], s_recv.at[h, g], partner
            ).wait_recv()
            for d in range(lo, hi):
                add_slots(h, d, acc)
        add_slots(h, 0, acc)
        for t in range(OWNED):
            out_ref[t, h * ROWS : (h + 1) * ROWS, :] = acc[t].astype(BF16)

    def add_slots(h, d, acc):
        for q in range(CAP):
            blk = slot_in[h, d, q].astype(F32)
            lab = jnp.broadcast_to(labels[d % NZ, d // NZ, 2 + q : 3 + q, :], (ROWS, 128))
            lab = jnp.concatenate([lab, lab], axis=1)
            for t in range(OWNED):
                acc[t] = acc[t] + jnp.where(lab == t, blk, 0.0)

    for cp in loads[:7]:
        cp.wait()
    for p in range(PAIRS):
        dcol[p] = jnp.full((128,), dest_s[p], I32)
        tcol[p] = jnp.full((128,), tgt_s[p], I32)
    lane = lax.broadcasted_iota(I32, (PAIRS, 128), 1)
    prow = lax.broadcasted_iota(I32, (PAIRS, 128), 0)
    same = dcol[...] == lane
    low = jnp.min(jnp.where(same, prow, PAIRS), axis=0, keepdims=True)
    high = jnp.max(jnp.where(same, prow, -1), axis=0, keepdims=True)
    low_t = jnp.max(jnp.where(same & (prow == low), tcol[...], -1), axis=0, keepdims=True)
    high_t = jnp.max(jnp.where(same & (prow == high) & (high > low), tcol[...], -1), axis=0, keepdims=True)
    tables[0, 0] = jnp.concatenate(
        [jnp.clip(low, 0, PAIRS - 1), jnp.clip(high, 0, PAIRS - 1), low_t, high_t, jnp.zeros((4, 128), I32)], axis=0
    )
    to_smem = pltpu.make_async_copy(tables.at[0, 0], table_s, table_sem)
    to_smem.start()
    loads[7].wait()

    compute(0)
    to_smem.wait()
    pl.semaphore_wait(barrier, 1 + NX - 1 + NS - 1)
    core_copy(0, 0).start()
    core_copy(1, 0).start()

    def ty_copy(d):
        return remote(tables.at[0, 0], tables.at[0, d], ty_send, ty_recv.at[d], at_s(d * NZ))

    def tz_copy(d):
        return remote(tables.at[0], tables.at[d], tz_send, tz_recv.at[d], at_s(d))

    for d in range(1, NY):
        ty_copy(d).start()

    def loop(b, _):
        compute(b)
        core_copy(0, b).start()
        core_copy(1, b).start()
        stage_x(0, b - 1)

        @pl.when(b == 2)
        def _():
            for d in range(1, NY):
                ty_copy(d).wait_recv()
            for d in range(1, NZ):
                tz_copy(d).start()

        return 0

    lax.fori_loop(1, NB, loop, 0)
    stage_sum(0, 0)
    stage_x(0, NB - 1)
    for b in range(NB):
        stage_x(1, b)
    for d in range(1, NZ):
        tz_copy(d).wait_recv()
    mine = lax.broadcasted_iota(I32, tables.shape, 3) == sector
    picked = jnp.sum(jnp.where(mine, tables[...], 0), axis=3, keepdims=True)
    labels[...] = jnp.broadcast_to(picked, tables.shape)
    for b in range(1, NB):
        stage_sum(0, b)
    send_slots(0)
    for b in range(NB):
        stage_sum(1, b)
    send_slots(1)
    finish(0)
    finish(1)

    remote(tables.at[0, 1:], tables.at[0, 1:], ty_send, ty_recv.at[1], partner).wait_send()
    remote(tables.at[1:], tables.at[1:], tz_send, tz_recv.at[1], partner).wait_send()
    for h in range(2):
        remote(core_in.at[h], core_in.at[h], core_send.at[h], core_recv.at[h, 0], partner).wait_send()
        remote(x_out.at[h], x_in.at[h], x_send.at[h], x_recv.at[h, 0], partner).wait_send()
        remote(slot_out.at[h, 1:], slot_in.at[h, 1:], s_send.at[h], s_recv.at[h, 0], partner).wait_send()


def shards(psi, left_env, right_env, pair_source, pair_left, pair_right, pair_dest, pair_target):
    block = (ROWS, WIDTH)
    dma = pltpu.SemaphoreType.DMA
    return pl.pallas_call(
        kernel,
        out_shape=jax.ShapeDtypeStruct((OWNED, 2 * ROWS, WIDTH), BF16),
        in_specs=[pl.BlockSpec(memory_space=pl.ANY)] * 8,
        out_specs=pl.BlockSpec(memory_space=pltpu.VMEM),
        scratch_shapes=[
            pltpu.VMEM((OWNED, WIDTH, WIDTH), BF16),
            pltpu.VMEM((4, TERMS, WIDTH, WIDTH), BF16),
            pltpu.VMEM((4, TERMS, WIDTH, WIDTH), BF16),
        ]
        + [pltpu.SMEM((PAIRS,), I32)] * 5
        + [
            pltpu.VMEM((BATCH, TERMS, WIDTH, WIDTH), BF16),
            pltpu.VMEM((2, NCORE, NB, NX, BATCH) + block, BF16),
            pltpu.VMEM((2, NB, NX, BATCH) + block, BF16),
            pltpu.VMEM((2, NB, NX - 1, BATCH) + block, BF16),
            pltpu.VMEM((2, NB, NX - 1, BATCH) + block, BF16),
            pltpu.VMEM((2, PAIRS) + block, BF16),
            pltpu.VMEM((2, NS, CAP) + block, BF16),
            pltpu.VMEM((2, NS, CAP) + block, BF16),
            pltpu.VMEM((PAIRS, 128), I32),
            pltpu.VMEM((PAIRS, 128), I32),
            pltpu.SMEM((8, 128), I32),
            pltpu.VMEM((NZ, NY, 8, 128), I32),
            pltpu.VMEM((NZ, NY, 8, 128), I32),
            dma((8,)), dma, dma, dma((NY,)), dma, dma((NZ,)),
            dma((2,)), dma((2, NB)),
            dma((2,)), dma((2, NB)),
            dma((2,)), dma((2, len(GROUPS))),
        ],
        compiler_params=pltpu.CompilerParams(
            collective_id=0, has_side_effects=True, vmem_limit_bytes=56 * 2**20
        ),
        name="sigma",
    )(
        psi,
        left_env.reshape((4, TERMS, WIDTH, WIDTH)),
        right_env.reshape((4, TERMS, WIDTH, WIDTH)),
        pair_source, pair_left, pair_right, pair_dest.reshape(PAIRS), pair_target,
    )


def solution(mesh):
    placed = (
        P("sector", None, None),
        P("term", "sector", None, None, None),
        P("term", "sector", None, None, None),
        P("sector"),
        P("sector"),
        P("sector"),
        P("sector", None),
        P("sector"),
    )
    return jax.shard_map(
        shards, mesh=mesh, in_specs=placed, out_specs=P("sector", "term", None), check_vma=False
    )
```

```python
import jax
import jax.numpy as jnp
from jax import lax
from jax.experimental import pallas as pl
from jax.experimental.pallas import tpu as pltpu
from jax.sharding import PartitionSpec as P

MESH = pl.DeviceIdType.MESH
F32, BF16, I32 = jnp.float32, jnp.bfloat16, jnp.int32

NX, NCORE, NY, NZ = 4, 2, 4, 8
PAIRS, TERMS, OWNED, WIDTH = 32, 4, 8, 256
ROWS, COLS, CHUNKS = 16, 128, 4
BATCH = 4
NB = PAIRS // BATCH
SUB = BATCH // 2
CAP = 2
LEFT, RIGHT = 0, 1
BOTH = (LEFT, RIGHT)
HALF_T = OWNED // 2


def kernel(
    psi_hbm, left_hbm, right_hbm, src_hbm, lft_hbm, rgt_hbm, dest_hbm, tgt_hbm,
    out_ref,
    psi, lenv, renv, src_s, lft_s, rgt_s, dest_s, tgt_s,
    inner, part, core_in, x_out, x_in, a_out, a_in, b_out, b_in, red,
    zslot_out, zslot_in, own, row_out, row_in, slot_out, slot_in, dens, near_out, near_in, far_out, far_in, mid_out, mid_in,
    dcol, tcol, table_s, tables, tables_z, labels, labels_z,
    load_sem, table_sem, table_send, table_recv, table_z_send, table_z_recv,
    core_send, core_recv, x_send, x_recv, a_send, a_recv, b_send, b_recv,
    zs_send, zs_recv, row_send, row_recv, y_send, y_recv, near_send, near_recv, far_send, far_recv, mid_send, mid_recv,
):
    term, sector = lax.axis_index("term"), lax.axis_index("sector")
    x, c = term // NCORE, term % NCORE
    y, z = sector // NZ, sector % NZ
    x_at = [lax.rem(x + d, NX) for d in range(NX)]
    y_at = [lax.rem(y + d, NY) * NZ for d in range(NY)]
    z_at = [lax.rem(z + d, NZ) for d in range(NZ)]

    def at_x(d):
        return (x_at[d] * NCORE + c, sector)

    def at_y(d):
        return (term, y_at[d] + z)

    def at_z(d):
        return (term, y_at[0] + z_at[d])

    partner = (x * NCORE + 1 - c, sector)
    x_dev = (at_x(3), at_x(1))
    z_one = (at_z(7), at_z(1))
    z_two = (at_z(6), at_z(2))

    small = [(src_hbm, src_s), (lft_hbm, lft_s), (rgt_hbm, rgt_s), (dest_hbm, dest_s), (tgt_hbm, tgt_s)]
    loads = small + [(psi_hbm, psi), (right_hbm, renv), (left_hbm, lenv)]
    loads = [pltpu.make_async_copy(a, b, load_sem.at[i]) for i, (a, b) in enumerate(loads)]
    for cp in loads:
        cp.start()

    barrier = pltpu.get_barrier_semaphore()
    peers = [partner] + [at_x(d) for d in (1, 2, 3)] + [at_y(d) for d in (1, 2, 3)]
    peers += [at_z(d) for d in range(1, NZ)]
    for dev in peers:
        pl.semaphore_signal(barrier, inc=1, device_id=dev, device_id_type=MESH)

    def remote(src, dst, send, recv, dev):
        return pltpu.make_async_remote_copy(
            src_ref=src, dst_ref=dst, send_sem=send, recv_sem=recv, device_id=dev, device_id_type=MESH
        )

    def arrived(dst, recv):
        remote(dst, dst, recv, recv, partner).wait_recv()

    def left(src, send):
        remote(src, src, send, send, partner).wait_send()

    def compute(b):
        for k in range(TERMS):
            for j in range(BATCH):
                p = b * BATCH + j
                inner[j, k] = jnp.dot(psi[src_s[p]], renv[rgt_s[p], k], preferred_element_type=F32).astype(BF16)
        for j in range(BATCH):
            l = lft_s[b * BATCH + j]
            acc = None
            for k in range(TERMS):
                d = jnp.dot(lenv[l, k], inner[j, k], preferred_element_type=F32)
                acc = d if acc is None else acc + d
            for xx in range(NX):
                for cc in range(NCORE):
                    for h in range(2):
                        r = ((xx * NCORE + cc) * 2 + h) * ROWS
                        part[h, cc, b, xx, j] = acc[r : r + ROWS].astype(BF16)

    def core_copy(h, b):
        return remote(part.at[h, 1 - c, b], core_in.at[h, b], core_send, core_recv.at[h, b], partner)

    def chip_sum(h, b, d, lo=0, hi=BATCH):
        xx = x_at[d]
        return part[h, c, b, xx, lo:hi].astype(F32) + core_in[h, b, xx, lo:hi].astype(F32)

    def x_copy(b, d):
        return remote(x_out.at[b, d - 1], x_in.at[b, d - 1], x_send, x_recv.at[b], at_x(d))

    def stage_x(b):
        arrived(core_in.at[0, b], core_recv.at[0, b])
        for d in (2, 1, 3):
            x_out[b, d - 1] = chip_sum(0, b, d).astype(BF16)
            x_copy(b, d).start()

    def stage_sum0(b):
        arrived(x_in.at[b], x_recv.at[b])
        total = chip_sum(0, b, 0)
        for d in (1, 2, 3):
            total = total + x_in[b, d - 1].astype(F32)
        red[0, pl.ds(b * BATCH, BATCH)] = total.astype(BF16)

    def stage_a(b):
        arrived(core_in.at[1, b], core_recv.at[1, b])
        for d in BOTH:
            a_out[b, d] = chip_sum(1, b, 2, d * SUB, (d + 1) * SUB).astype(BF16)
            remote(a_out.at[b, d], a_in.at[b, d], a_send, a_recv.at[b], x_dev[d]).start()

    def send_b(ch, lo, hi):
        for d in BOTH:
            ps = pl.ds(lo * BATCH, (hi - lo) * BATCH)
            remote(b_out.at[ch, d, ps], b_in.at[ch, d, ps], b_send, b_recv.at[ch], x_dev[d]).start()

    def stage_b(b):
        arrived(a_in.at[b], a_recv.at[b])
        for d in BOTH:
            total = chip_sum(1, b, 3 if d == LEFT else 1)
            extra = a_in[b, d].astype(F32)
            lo, hi = total[:SUB], total[SUB:]
            if d == LEFT:
                lo = lo + extra
            else:
                hi = hi + extra
            total = jnp.concatenate([lo, hi], axis=0).astype(BF16)
            for ch in range(2):
                b_out[ch, d, pl.ds(b * BATCH, BATCH)] = total[:, :, ch * COLS : (ch + 1) * COLS]

    def stage_sum1(ch):
        arrived(b_in.at[ch], b_recv.at[ch])
        cols = slice(ch * COLS, (ch + 1) * COLS)
        for b in range(NB):
            ps = pl.ds(b * BATCH, BATCH)
            xx = x_at[0]
            total = part[1, c, b, xx, :, :, cols].astype(F32) + core_in[1, b, xx, :, :, cols].astype(F32)
            total = total + b_in[ch, LEFT, ps].astype(F32) + b_in[ch, RIGHT, ps].astype(F32)
            red[1, ps, :, cols] = total.astype(BF16)

    def add_slot(acc, blk, lab):
        blk = blk.astype(F32)
        lab = jnp.broadcast_to(lab, (ROWS, COLS))
        for t in range(OWNED):
            term_ = jnp.where(lab == t, blk, 0.0)
            acc[t] = term_ if acc[t] is None else acc[t] + term_

    def send_z():
        for dz in (4, 3, 5, 2, 6, 1, 7, 0):
            for dy in range(NY):
                o = y_at[dy] + z_at[dz]
                for s in range(CAP):
                    blk = red[0, table_s[s, o], :, :COLS]
                    if dz:
                        zslot_out[dz - 1, dy, s] = blk
                    else:
                        zslot_in[0, dy, s] = blk
            if dz:
                remote(zslot_out.at[dz - 1], zslot_in.at[dz], zs_send, zs_recv, at_z(dz)).start()

    def row_z():
        arrived(zslot_in.at[1:], zs_recv)
        for dy in (2, 1, 3, 0):
            acc = [None] * OWNED
            for dz in range(NZ):
                for s in range(CAP):
                    add_slot(acc, zslot_in[dz, dy, s], labels_z[dy, dz, 2 + s : 3 + s, :])
            for t in range(OWNED):
                if dy:
                    row_out[dy - 1, t] = acc[t].astype(BF16)
                else:
                    own[t] = acc[t]
            if dy:
                remote(row_out.at[dy - 1], row_in.at[dy - 1], row_send, row_recv, at_y(dy)).start()

    def finish_z():
        arrived(row_in, row_recv)
        total = own[...]
        for dy in range(1, NY):
            total = total + row_in[dy - 1].astype(F32)
        out_ref[:, :ROWS, :COLS] = total.astype(BF16)

    def send_y(q):
        h, cols = q // 2, slice((q % 2) * COLS, (q % 2 + 1) * COLS)
        for dy in (2, 1, 3, 0):
            for dz in range(NZ):
                o = y_at[dy] + z_at[dz]
                for s in range(CAP):
                    blk = red[h, table_s[s, o], :, cols]
                    if dy:
                        slot_out[q - 1, dy - 1, dz, s] = blk
                    else:
                        slot_in[q - 1, 0, dz, s] = blk
            if dy:
                remote(slot_out.at[q - 1, dy - 1], slot_in.at[q - 1, dy], y_send, y_recv.at[q - 1], at_y(dy)).start()

    def dense(q, dz):
        acc = [None] * OWNED
        for dy in range(NY):
            for s in range(CAP):
                add_slot(acc, slot_in[q - 1, dy, dz, s], labels[dz, dy, 2 + s : 3 + s, :])
        return acc

    def first_z(q):
        arrived(slot_in.at[q - 1, 1:], y_recv.at[q - 1])
        acc = dense(q, 4)
        for t in range(HALF_T):
            far_out[q - 1, RIGHT, t] = acc[t].astype(BF16)
            far_out[q - 1, LEFT, t] = acc[HALF_T + t].astype(BF16)
        for d in BOTH:
            remote(far_out.at[q - 1, d], far_in.at[q - 1, d], far_send, far_recv.at[q - 1, d], z_two[d]).start()
        for d in BOTH:
            for i, dz in enumerate((1, 3) if d == RIGHT else (7, 5)):
                acc = dense(q, dz)
                for t in range(OWNED):
                    near_out[q - 1, d, i, t] = acc[t].astype(BF16)
            remote(near_out.at[q - 1, d], near_in.at[q - 1, d], near_send, near_recv.at[q - 1, d], z_one[d]).start()
        for i, dz in enumerate((6, 2, 0)):
            acc = dense(q, dz)
            for t in range(OWNED):
                dens[q - 1, i, t] = acc[t]

    def second_z(q):
        for d in BOTH:
            arrived(far_in.at[q - 1, d], far_recv.at[q - 1, d])
            arrived(near_in.at[q - 1, d], near_recv.at[q - 1, d])
            total = dens[q - 1, d] + near_in[q - 1, d, 1].astype(F32)
            far = far_in[q - 1, d].astype(F32)
            lo, hi = total[:HALF_T], total[HALF_T:]
            if d == RIGHT:
                lo = lo + far
            else:
                hi = hi + far
            mid_out[q - 1, d, :HALF_T] = lo.astype(BF16)
            mid_out[q - 1, d, HALF_T:] = hi.astype(BF16)
            remote(mid_out.at[q - 1, d], mid_in.at[q - 1, d], mid_send, mid_recv.at[q - 1, d], z_two[d]).start()

    def finish(q):
        h, cols = q // 2, slice((q % 2) * COLS, (q % 2 + 1) * COLS)
        total = dens[q - 1, 2]
        for d in BOTH:
            total = total + near_in[q - 1, d, 0].astype(F32)
        for d in BOTH:
            arrived(mid_in.at[q - 1, d], mid_recv.at[q - 1, d])
            total = total + mid_in[q - 1, d].astype(F32)
        out_ref[:, h * ROWS : (h + 1) * ROWS, cols] = total.astype(BF16)

    for cp in loads[:5]:
        cp.wait()
    for p in range(PAIRS):
        dcol[p] = jnp.full((128,), dest_s[p], I32)
        tcol[p] = jnp.full((128,), tgt_s[p], I32)
    lane = lax.broadcasted_iota(I32, (PAIRS, 128), 1)
    prow = lax.broadcasted_iota(I32, (PAIRS, 128), 0)
    same = dcol[...] == lane
    low = jnp.min(jnp.where(same, prow, PAIRS), axis=0, keepdims=True)
    high = jnp.max(jnp.where(same, prow, -1), axis=0, keepdims=True)
    low_t = jnp.max(jnp.where(same & (prow == low), tcol[...], -1), axis=0, keepdims=True)
    high_t = jnp.max(jnp.where(same & (prow == high) & (high > low), tcol[...], -1), axis=0, keepdims=True)
    tables[0] = jnp.concatenate(
        [jnp.clip(low, 0, PAIRS - 1), jnp.clip(high, 0, PAIRS - 1), low_t, high_t, jnp.zeros((4, 128), I32)], axis=0
    )
    to_smem = pltpu.make_async_copy(tables.at[0], table_s, table_sem)
    to_smem.start()
    for cp in loads[5:]:
        cp.wait()

    compute(0)
    to_smem.wait()
    pl.semaphore_wait(barrier, len(peers))
    core_copy(0, 0).start()
    core_copy(1, 0).start()
    for d in range(1, NY):
        remote(tables.at[0], tables.at[d], table_send, table_recv, at_y(d)).start()
    for d in range(1, NZ):
        remote(tables.at[0], tables_z.at[d], table_z_send, table_z_recv, at_z(d)).start()
    tables_z[0] = tables[0]

    def loop(b, _):
        compute(b)
        core_copy(0, b).start()
        core_copy(1, b).start()
        stage_x(b - 1)
        stage_a(b - 1)
        return 0

    lax.fori_loop(1, NB, loop, 0)
    stage_x(NB - 1)
    stage_a(NB - 1)
    for b in range(NB - 2):
        stage_b(b)
    send_b(0, 0, NB - 2)
    arrived(tables.at[1:], table_recv)
    arrived(tables_z.at[1:], table_z_recv)
    lane = lax.broadcasted_iota(I32, (NY, 8, 128), 2)
    for dz in range(NZ):
        mine = jnp.sum(jnp.where(lane == y_at[0] + z_at[dz], tables[...], 0), axis=2, keepdims=True)
        labels[dz] = jnp.broadcast_to(mine, (NY, 8, 128))
    lane = lax.broadcasted_iota(I32, (NZ, 8, 128), 2)
    for dy in range(NY):
        mine = jnp.sum(jnp.where(lane == y_at[dy] + z, tables_z[...], 0), axis=2, keepdims=True)
        labels_z[dy] = jnp.broadcast_to(mine, (NZ, 8, 128))
    for b in range(NB):
        stage_sum0(b)
    send_z()
    send_y(1)
    for b in range(NB - 2, NB):
        stage_b(b)
    send_b(0, NB - 2, NB)
    send_b(1, 0, NB)
    stage_sum1(0)
    send_y(2)
    first_z(1)
    stage_sum1(1)
    send_y(3)
    row_z()
    first_z(2)
    second_z(1)
    first_z(3)
    finish_z()
    second_z(2)
    finish(1)
    second_z(3)
    finish(2)
    finish(3)

    left(tables.at[1:], table_send)
    left(tables_z.at[1:], table_z_send)
    left(core_in, core_send)
    left(x_out, x_send)
    left(a_out, a_send)
    left(b_out, b_send)
    left(zslot_out, zs_send)
    left(row_out, row_send)
    left(slot_out, y_send)
    left(near_out, near_send)
    left(far_out, far_send)
    left(mid_out, mid_send)


def shards(psi, left_env, right_env, pair_source, pair_left, pair_right, pair_dest, pair_target):
    block, tile = (ROWS, WIDTH), (ROWS, COLS)
    dma = pltpu.SemaphoreType.DMA
    return pl.pallas_call(
        kernel,
        out_shape=jax.ShapeDtypeStruct((OWNED, 2 * ROWS, WIDTH), BF16),
        in_specs=[pl.BlockSpec(memory_space=pl.ANY)] * 8,
        out_specs=pl.BlockSpec(memory_space=pltpu.VMEM),
        scratch_shapes=[
            pltpu.VMEM((OWNED, WIDTH, WIDTH), BF16),
            pltpu.VMEM((4, TERMS, WIDTH, WIDTH), BF16),
            pltpu.VMEM((4, TERMS, WIDTH, WIDTH), BF16),
        ]
        + [pltpu.SMEM((PAIRS,), I32)] * 5
        + [
            pltpu.VMEM((BATCH, TERMS, WIDTH, WIDTH), BF16),
            pltpu.VMEM((2, NCORE, NB, NX, BATCH) + block, BF16),
            pltpu.VMEM((2, NB, NX, BATCH) + block, BF16),
            pltpu.VMEM((NB, NX - 1, BATCH) + block, BF16),
            pltpu.VMEM((NB, NX - 1, BATCH) + block, BF16),
            pltpu.VMEM((NB, 2, SUB) + block, BF16),
            pltpu.VMEM((NB, 2, SUB) + block, BF16),
            pltpu.VMEM((2, 2, PAIRS) + tile, BF16),
            pltpu.VMEM((2, 2, PAIRS) + tile, BF16),
            pltpu.VMEM((2, PAIRS) + block, BF16),
            pltpu.VMEM((NZ - 1, NY, CAP) + tile, BF16),
            pltpu.VMEM((NZ, NY, CAP) + tile, BF16),
            pltpu.VMEM((OWNED,) + tile, F32),
            pltpu.VMEM((NY - 1, OWNED) + tile, BF16),
            pltpu.VMEM((NY - 1, OWNED) + tile, BF16),
            pltpu.VMEM((CHUNKS - 1, NY - 1, NZ, CAP) + tile, BF16),
            pltpu.VMEM((CHUNKS - 1, NY, NZ, CAP) + tile, BF16),
            pltpu.VMEM((CHUNKS - 1, 3, OWNED) + tile, F32),
            pltpu.VMEM((CHUNKS - 1, 2, 2, OWNED) + tile, BF16),
            pltpu.VMEM((CHUNKS - 1, 2, 2, OWNED) + tile, BF16),
            pltpu.VMEM((CHUNKS - 1, 2, HALF_T) + tile, BF16),
            pltpu.VMEM((CHUNKS - 1, 2, HALF_T) + tile, BF16),
            pltpu.VMEM((CHUNKS - 1, 2, OWNED) + tile, BF16),
            pltpu.VMEM((CHUNKS - 1, 2, OWNED) + tile, BF16),
            pltpu.VMEM((PAIRS, 128), I32),
            pltpu.VMEM((PAIRS, 128), I32),
            pltpu.SMEM((8, 128), I32),
            pltpu.VMEM((NY, 8, 128), I32),
            pltpu.VMEM((NZ, 8, 128), I32),
            pltpu.VMEM((NZ, NY, 8, 128), I32),
            pltpu.VMEM((NY, NZ, 8, 128), I32),
            dma((8,)), dma, dma, dma, dma, dma,
            dma, dma((2, NB)), dma, dma((NB,)), dma, dma((NB,)), dma, dma((2,)),
            dma, dma, dma, dma, dma, dma((CHUNKS - 1,)),
            dma, dma((CHUNKS - 1, 2)), dma, dma((CHUNKS - 1, 2)), dma, dma((CHUNKS - 1, 2)),
        ],
        compiler_params=pltpu.CompilerParams(
            collective_id=0, has_side_effects=True, vmem_limit_bytes=56 * 2**20
        ),
        name="sigma",
    )(
        psi,
        left_env.reshape((4, TERMS, WIDTH, WIDTH)),
        right_env.reshape((4, TERMS, WIDTH, WIDTH)),
        pair_source, pair_left, pair_right, pair_dest.reshape(PAIRS), pair_target,
    )


def solution(mesh):
    placed = (
        P("sector", None, None),
        P("term", "sector", None, None, None),
        P("term", "sector", None, None, None),
        P("sector"),
        P("sector"),
        P("sector"),
        P("sector", None),
        P("sector"),
    )
    return jax.shard_map(
        shards, mesh=mesh, in_specs=placed, out_specs=P("sector", "term", None), check_vma=False
    )
```

```python
import jax
import jax.numpy as jnp
from jax import lax
from jax.experimental import pallas as pl
from jax.experimental.pallas import tpu as pltpu
from jax.sharding import PartitionSpec as P

MESH = pl.DeviceIdType.MESH
F32, BF16, I32 = jnp.float32, jnp.bfloat16, jnp.int32

NX, NCORE, NY, NZ = 4, 2, 4, 8
PAIRS, TERMS, OWNED, WIDTH = 32, 4, 8, 256
ROWS, COLS, CHUNKS = 16, 128, 4
BATCH = 4
NB = PAIRS // BATCH
SUB = BATCH // 2
CAP = 2
LEFT, RIGHT = 0, 1
BOTH = (LEFT, RIGHT)
HALF_T = OWNED // 2


def kernel(
    psi_hbm, left_hbm, right_hbm, src_hbm, lft_hbm, rgt_hbm, dest_hbm, tgt_hbm,
    out_ref,
    psi, lenv, renv, src_s, lft_s, rgt_s, dest_s, tgt_s,
    inner, part, core_in, x_out, x_in, a_out, a_in, b_out, b_in, red,
    zslot_out, zslot_in, own, row_out, row_in, slot_out, slot_in, dens, near_out, near_in, far_out, far_in, mid_out, mid_in,
    dcol, tcol, table_s, tables, tables_z, labels, labels_z,
    load_sem, table_sem, table_send, table_recv, table_z_send, table_z_recv,
    core_send, core_recv, x_send, x_recv, a_send, a_recv, b_send, b_recv,
    zs_send, zs_recv, row_send, row_recv, y_send, y_recv, near_send, near_recv, far_send, far_recv, mid_send, mid_recv,
):
    term, sector = lax.axis_index("term"), lax.axis_index("sector")
    x, c = term // NCORE, term % NCORE
    y, z = sector // NZ, sector % NZ
    x_at = [lax.rem(x + d, NX) for d in range(NX)]
    y_at = [lax.rem(y + d, NY) * NZ for d in range(NY)]
    z_at = [lax.rem(z + d, NZ) for d in range(NZ)]

    def at_x(d):
        return (x_at[d] * NCORE + c, sector)

    def at_y(d):
        return (term, y_at[d] + z)

    def at_z(d):
        return (term, y_at[0] + z_at[d])

    partner = (x * NCORE + 1 - c, sector)
    x_dev = (at_x(3), at_x(1))
    z_one = (at_z(7), at_z(1))
    z_two = (at_z(6), at_z(2))

    small = [(src_hbm, src_s), (lft_hbm, lft_s), (rgt_hbm, rgt_s), (dest_hbm, dest_s), (tgt_hbm, tgt_s)]
    loads = small + [(psi_hbm, psi), (right_hbm, renv), (left_hbm, lenv)]
    loads = [pltpu.make_async_copy(a, b, load_sem.at[i]) for i, (a, b) in enumerate(loads)]
    for cp in loads:
        cp.start()

    barrier = pltpu.get_barrier_semaphore()
    peers = [partner] + [at_x(d) for d in (1, 2, 3)] + [at_y(d) for d in (1, 2, 3)]
    peers += [at_z(d) for d in range(1, NZ)]
    for dev in peers:
        pl.semaphore_signal(barrier, inc=1, device_id=dev, device_id_type=MESH)

    def remote(src, dst, send, recv, dev):
        return pltpu.make_async_remote_copy(
            src_ref=src, dst_ref=dst, send_sem=send, recv_sem=recv, device_id=dev, device_id_type=MESH
        )

    def arrived(dst, recv):
        remote(dst, dst, recv, recv, partner).wait_recv()

    def left(src, send):
        remote(src, src, send, send, partner).wait_send()

    def compute(b):
        for k in range(TERMS):
            for j in range(BATCH):
                p = b * BATCH + j
                inner[j, k] = jnp.dot(psi[src_s[p]], renv[rgt_s[p], k], preferred_element_type=F32).astype(BF16)
        for j in range(BATCH):
            l = lft_s[b * BATCH + j]
            acc = None
            for k in range(TERMS):
                d = jnp.dot(lenv[l, k], inner[j, k], preferred_element_type=F32)
                acc = d if acc is None else acc + d
            for xx in range(NX):
                for cc in range(NCORE):
                    for h in range(2):
                        r = ((xx * NCORE + cc) * 2 + h) * ROWS
                        part[h, cc, b, xx, j] = acc[r : r + ROWS].astype(BF16)

    def core_copy(h, b):
        return remote(part.at[h, 1 - c, b], core_in.at[h, b], core_send, core_recv.at[h, b], partner)

    def chip_sum(h, b, d, lo=0, hi=BATCH):
        xx = x_at[d]
        return part[h, c, b, xx, lo:hi].astype(F32) + core_in[h, b, xx, lo:hi].astype(F32)

    def x_copy(b, d):
        return remote(x_out.at[b, d - 1], x_in.at[b, d - 1], x_send, x_recv.at[b], at_x(d))

    def stage_x(b):
        arrived(core_in.at[0, b], core_recv.at[0, b])
        for d in (2, 1, 3):
            x_out[b, d - 1] = chip_sum(0, b, d).astype(BF16)
            x_copy(b, d).start()

    def stage_sum0(b):
        arrived(x_in.at[b], x_recv.at[b])
        total = chip_sum(0, b, 0)
        for d in (1, 2, 3):
            total = total + x_in[b, d - 1].astype(F32)
        red[0, pl.ds(b * BATCH, BATCH)] = total.astype(BF16)

    def stage_a(b):
        arrived(core_in.at[1, b], core_recv.at[1, b])
        for d in BOTH:
            a_out[b, d] = chip_sum(1, b, 2, d * SUB, (d + 1) * SUB).astype(BF16)
            remote(a_out.at[b, d], a_in.at[b, d], a_send, a_recv.at[b], x_dev[d]).start()

    def send_b(ch, lo, hi):
        for d in BOTH:
            ps = pl.ds(lo * BATCH, (hi - lo) * BATCH)
            remote(b_out.at[ch, d, ps], b_in.at[ch, d, ps], b_send, b_recv.at[ch], x_dev[d]).start()

    def stage_b(b):
        arrived(a_in.at[b], a_recv.at[b])
        for d in BOTH:
            total = chip_sum(1, b, 3 if d == LEFT else 1)
            extra = a_in[b, d].astype(F32)
            lo, hi = total[:SUB], total[SUB:]
            if d == LEFT:
                lo = lo + extra
            else:
                hi = hi + extra
            total = jnp.concatenate([lo, hi], axis=0).astype(BF16)
            for ch in range(2):
                b_out[ch, d, pl.ds(b * BATCH, BATCH)] = total[:, :, ch * COLS : (ch + 1) * COLS]

    def stage_sum1(ch):
        arrived(b_in.at[ch], b_recv.at[ch])
        cols = slice(ch * COLS, (ch + 1) * COLS)
        for b in range(NB):
            ps = pl.ds(b * BATCH, BATCH)
            xx = x_at[0]
            total = part[1, c, b, xx, :, :, cols].astype(F32) + core_in[1, b, xx, :, :, cols].astype(F32)
            total = total + b_in[ch, LEFT, ps].astype(F32) + b_in[ch, RIGHT, ps].astype(F32)
            red[1, ps, :, cols] = total.astype(BF16)

    def add_slot(acc, blk, lab):
        blk = blk.astype(F32)
        lab = jnp.broadcast_to(lab, (ROWS, COLS))
        for t in range(OWNED):
            term_ = jnp.where(lab == t, blk, 0.0)
            acc[t] = term_ if acc[t] is None else acc[t] + term_

    def send_z(q):
        h, i, cols = q // 2, q, slice((q % 2) * COLS, (q % 2 + 1) * COLS)
        for dz in (4, 3, 5, 2, 6, 1, 7, 0):
            for dy in range(NY):
                o = y_at[dy] + z_at[dz]
                for s in range(CAP):
                    blk = red[h, table_s[s, o], :, cols]
                    if dz:
                        zslot_out[i, dz - 1, dy, s] = blk
                    else:
                        zslot_in[i, 0, dy, s] = blk
            if dz:
                remote(
                    zslot_out.at[i, dz - 1], zslot_in.at[i, dz], zs_send.at[i], zs_recv.at[i], at_z(dz)
                ).start()

    def row_z(q):
        i = q
        arrived(zslot_in.at[i, 1:], zs_recv.at[i])
        for dy in (2, 1, 3, 0):
            acc = [None] * OWNED
            for dz in range(NZ):
                for s in range(CAP):
                    add_slot(acc, zslot_in[i, dz, dy, s], labels_z[dy, dz, 2 + s : 3 + s, :])
            for t in range(OWNED):
                if dy:
                    row_out[i, dy - 1, t] = acc[t].astype(BF16)
                else:
                    own[i, t] = acc[t]
            if dy:
                remote(
                    row_out.at[i, dy - 1], row_in.at[i, dy - 1], row_send.at[i], row_recv.at[i], at_y(dy)
                ).start()

    def finish_z(q):
        h, i, cols = q // 2, q, slice((q % 2) * COLS, (q % 2 + 1) * COLS)
        arrived(row_in.at[i], row_recv.at[i])
        total = own[i]
        for dy in range(1, NY):
            total = total + row_in[i, dy - 1].astype(F32)
        out_ref[:, h * ROWS : (h + 1) * ROWS, cols] = total.astype(BF16)

    def send_y(q):
        h, cols = q // 2, slice((q % 2) * COLS, (q % 2 + 1) * COLS)
        for dy in (2, 1, 3, 0):
            for dz in range(NZ):
                o = y_at[dy] + z_at[dz]
                for s in range(CAP):
                    blk = red[h, table_s[s, o], :, cols]
                    if dy:
                        slot_out[q - 2, dy - 1, dz, s] = blk
                    else:
                        slot_in[q - 2, 0, dz, s] = blk
            if dy:
                remote(slot_out.at[q - 2, dy - 1], slot_in.at[q - 2, dy], y_send, y_recv.at[q - 2], at_y(dy)).start()

    def dense(q, dz):
        acc = [None] * OWNED
        for dy in range(NY):
            for s in range(CAP):
                add_slot(acc, slot_in[q - 2, dy, dz, s], labels[dz, dy, 2 + s : 3 + s, :])
        return acc

    def first_z(q):
        arrived(slot_in.at[q - 2, 1:], y_recv.at[q - 2])
        acc = dense(q, 4)
        for t in range(HALF_T):
            far_out[q - 2, RIGHT, t] = acc[t].astype(BF16)
            far_out[q - 2, LEFT, t] = acc[HALF_T + t].astype(BF16)
        for d in BOTH:
            remote(far_out.at[q - 2, d], far_in.at[q - 2, d], far_send, far_recv.at[q - 2, d], z_two[d]).start()
        for d in BOTH:
            for i, dz in enumerate((1, 3) if d == RIGHT else (7, 5)):
                acc = dense(q, dz)
                for t in range(OWNED):
                    near_out[q - 2, d, i, t] = acc[t].astype(BF16)
            remote(near_out.at[q - 2, d], near_in.at[q - 2, d], near_send, near_recv.at[q - 2, d], z_one[d]).start()
        for i, dz in enumerate((6, 2, 0)):
            acc = dense(q, dz)
            for t in range(OWNED):
                dens[q - 2, i, t] = acc[t]

    def second_z(q):
        for d in BOTH:
            arrived(far_in.at[q - 2, d], far_recv.at[q - 2, d])
            arrived(near_in.at[q - 2, d], near_recv.at[q - 2, d])
            total = dens[q - 2, d] + near_in[q - 2, d, 1].astype(F32)
            far = far_in[q - 2, d].astype(F32)
            lo, hi = total[:HALF_T], total[HALF_T:]
            if d == RIGHT:
                lo = lo + far
            else:
                hi = hi + far
            mid_out[q - 2, d, :HALF_T] = lo.astype(BF16)
            mid_out[q - 2, d, HALF_T:] = hi.astype(BF16)
            remote(mid_out.at[q - 2, d], mid_in.at[q - 2, d], mid_send, mid_recv.at[q - 2, d], z_two[d]).start()

    def finish(q):
        h, cols = q // 2, slice((q % 2) * COLS, (q % 2 + 1) * COLS)
        total = dens[q - 2, 2]
        for d in BOTH:
            total = total + near_in[q - 2, d, 0].astype(F32)
        for d in BOTH:
            arrived(mid_in.at[q - 2, d], mid_recv.at[q - 2, d])
            total = total + mid_in[q - 2, d].astype(F32)
        out_ref[:, h * ROWS : (h + 1) * ROWS, cols] = total.astype(BF16)

    for cp in loads[:5]:
        cp.wait()
    for p in range(PAIRS):
        dcol[p] = jnp.full((128,), dest_s[p], I32)
        tcol[p] = jnp.full((128,), tgt_s[p], I32)
    lane = lax.broadcasted_iota(I32, (PAIRS, 128), 1)
    prow = lax.broadcasted_iota(I32, (PAIRS, 128), 0)
    same = dcol[...] == lane
    low = jnp.min(jnp.where(same, prow, PAIRS), axis=0, keepdims=True)
    high = jnp.max(jnp.where(same, prow, -1), axis=0, keepdims=True)
    low_t = jnp.max(jnp.where(same & (prow == low), tcol[...], -1), axis=0, keepdims=True)
    high_t = jnp.max(jnp.where(same & (prow == high) & (high > low), tcol[...], -1), axis=0, keepdims=True)
    tables[0] = jnp.concatenate(
        [jnp.clip(low, 0, PAIRS - 1), jnp.clip(high, 0, PAIRS - 1), low_t, high_t, jnp.zeros((4, 128), I32)], axis=0
    )
    to_smem = pltpu.make_async_copy(tables.at[0], table_s, table_sem)
    to_smem.start()
    for cp in loads[5:]:
        cp.wait()

    compute(0)
    to_smem.wait()
    pl.semaphore_wait(barrier, len(peers))
    core_copy(0, 0).start()
    core_copy(1, 0).start()
    def send_tables():
        for d in range(1, NY):
            remote(tables.at[0], tables.at[d], table_send, table_recv, at_y(d)).start()
        for d in range(1, NZ):
            remote(tables.at[0], tables_z.at[d], table_z_send, table_z_recv, at_z(d)).start()
        tables_z[0] = tables[0]

    def loop(b, _):
        compute(b)
        core_copy(0, b).start()
        core_copy(1, b).start()
        stage_x(b - 1)
        stage_a(b - 1)

        @pl.when(b == 2)
        def _():
            send_tables()

        return 0

    lax.fori_loop(1, NB, loop, 0)
    stage_x(NB - 1)
    stage_a(NB - 1)
    for b in range(NB - 2):
        stage_b(b)
    send_b(0, 0, NB - 2)
    arrived(tables.at[1:], table_recv)
    arrived(tables_z.at[1:], table_z_recv)
    lane = lax.broadcasted_iota(I32, (NY, 8, 128), 2)
    for dz in range(NZ):
        mine = jnp.sum(jnp.where(lane == y_at[0] + z_at[dz], tables[...], 0), axis=2, keepdims=True)
        labels[dz] = jnp.broadcast_to(mine, (NY, 8, 128))
    lane = lax.broadcasted_iota(I32, (NZ, 8, 128), 2)
    for dy in range(NY):
        mine = jnp.sum(jnp.where(lane == y_at[dy] + z, tables_z[...], 0), axis=2, keepdims=True)
        labels_z[dy] = jnp.broadcast_to(mine, (NZ, 8, 128))
    for b in range(NB):
        stage_sum0(b)
    send_z(0)
    send_z(1)
    for b in range(NB - 2, NB):
        stage_b(b)
    send_b(0, NB - 2, NB)
    send_b(1, 0, NB)
    stage_sum1(0)
    send_y(2)
    stage_sum1(1)
    send_y(3)
    row_z(0)
    first_z(2)
    first_z(3)
    row_z(1)
    second_z(2)
    finish_z(0)
    second_z(3)
    finish_z(1)
    finish(2)
    finish(3)

    left(tables.at[1:], table_send)
    left(tables_z.at[1:], table_z_send)
    left(core_in, core_send)
    left(x_out, x_send)
    left(a_out, a_send)
    left(b_out, b_send)
    for i in range(2):
        left(zslot_out.at[i], zs_send.at[i])
        left(row_out.at[i], row_send.at[i])
    left(slot_out, y_send)
    left(near_out, near_send)
    left(far_out, far_send)
    left(mid_out, mid_send)


def shards(psi, left_env, right_env, pair_source, pair_left, pair_right, pair_dest, pair_target):
    block, tile = (ROWS, WIDTH), (ROWS, COLS)
    dma = pltpu.SemaphoreType.DMA
    return pl.pallas_call(
        kernel,
        out_shape=jax.ShapeDtypeStruct((OWNED, 2 * ROWS, WIDTH), BF16),
        in_specs=[pl.BlockSpec(memory_space=pl.ANY)] * 8,
        out_specs=pl.BlockSpec(memory_space=pltpu.VMEM),
        scratch_shapes=[
            pltpu.VMEM((OWNED, WIDTH, WIDTH), BF16),
            pltpu.VMEM((4, TERMS, WIDTH, WIDTH), BF16),
            pltpu.VMEM((4, TERMS, WIDTH, WIDTH), BF16),
        ]
        + [pltpu.SMEM((PAIRS,), I32)] * 5
        + [
            pltpu.VMEM((BATCH, TERMS, WIDTH, WIDTH), BF16),
            pltpu.VMEM((2, NCORE, NB, NX, BATCH) + block, BF16),
            pltpu.VMEM((2, NB, NX, BATCH) + block, BF16),
            pltpu.VMEM((NB, NX - 1, BATCH) + block, BF16),
            pltpu.VMEM((NB, NX - 1, BATCH) + block, BF16),
            pltpu.VMEM((NB, 2, SUB) + block, BF16),
            pltpu.VMEM((NB, 2, SUB) + block, BF16),
            pltpu.VMEM((2, 2, PAIRS) + tile, BF16),
            pltpu.VMEM((2, 2, PAIRS) + tile, BF16),
            pltpu.VMEM((2, PAIRS) + block, BF16),
            pltpu.VMEM((2, NZ - 1, NY, CAP) + tile, BF16),
            pltpu.VMEM((2, NZ, NY, CAP) + tile, BF16),
            pltpu.VMEM((2, OWNED) + tile, F32),
            pltpu.VMEM((2, NY - 1, OWNED) + tile, BF16),
            pltpu.VMEM((2, NY - 1, OWNED) + tile, BF16),
            pltpu.VMEM((CHUNKS - 2, NY - 1, NZ, CAP) + tile, BF16),
            pltpu.VMEM((CHUNKS - 2, NY, NZ, CAP) + tile, BF16),
            pltpu.VMEM((CHUNKS - 2, 3, OWNED) + tile, F32),
            pltpu.VMEM((CHUNKS - 2, 2, 2, OWNED) + tile, BF16),
            pltpu.VMEM((CHUNKS - 2, 2, 2, OWNED) + tile, BF16),
            pltpu.VMEM((CHUNKS - 2, 2, HALF_T) + tile, BF16),
            pltpu.VMEM((CHUNKS - 2, 2, HALF_T) + tile, BF16),
            pltpu.VMEM((CHUNKS - 2, 2, OWNED) + tile, BF16),
            pltpu.VMEM((CHUNKS - 2, 2, OWNED) + tile, BF16),
            pltpu.VMEM((PAIRS, 128), I32),
            pltpu.VMEM((PAIRS, 128), I32),
            pltpu.SMEM((8, 128), I32),
            pltpu.VMEM((NY, 8, 128), I32),
            pltpu.VMEM((NZ, 8, 128), I32),
            pltpu.VMEM((NZ, NY, 8, 128), I32),
            pltpu.VMEM((NY, NZ, 8, 128), I32),
            dma((8,)), dma, dma, dma, dma, dma,
            dma, dma((2, NB)), dma, dma((NB,)), dma, dma((NB,)), dma, dma((2,)),
            dma((2,)), dma((2,)), dma((2,)), dma((2,)), dma, dma((CHUNKS - 2,)),
            dma, dma((CHUNKS - 2, 2)), dma, dma((CHUNKS - 2, 2)), dma, dma((CHUNKS - 2, 2)),
        ],
        compiler_params=pltpu.CompilerParams(
            collective_id=0, has_side_effects=True, vmem_limit_bytes=56 * 2**20
        ),
        name="sigma",
    )(
        psi,
        left_env.reshape((4, TERMS, WIDTH, WIDTH)),
        right_env.reshape((4, TERMS, WIDTH, WIDTH)),
        pair_source, pair_left, pair_right, pair_dest.reshape(PAIRS), pair_target,
    )


def solution(mesh):
    placed = (
        P("sector", None, None),
        P("term", "sector", None, None, None),
        P("term", "sector", None, None, None),
        P("sector"),
        P("sector"),
        P("sector"),
        P("sector", None),
        P("sector"),
    )
    return jax.shard_map(
        shards, mesh=mesh, in_specs=placed, out_specs=P("sector", "term", None), check_vma=False
    )
```

```python
import jax
import jax.numpy as jnp
from jax import lax
from jax.experimental import pallas as pl
from jax.experimental.pallas import tpu as pltpu
from jax.sharding import PartitionSpec as P

MESH = pl.DeviceIdType.MESH
F32, BF16, I32 = jnp.float32, jnp.bfloat16, jnp.int32

NX, NCORE, NY, NZ = 4, 2, 4, 8
PAIRS, TERMS, OWNED, WIDTH = 32, 4, 8, 256
ROWS, COLS, CHUNKS = 16, 128, 4
BATCH = 4
NB = PAIRS // BATCH
SUB = BATCH // 2
CAP = 2
LEFT, RIGHT = 0, 1
BOTH = (LEFT, RIGHT)
HALF_T = OWNED // 2


def kernel(
    psi_hbm, left_hbm, right_hbm, src_hbm, lft_hbm, rgt_hbm, dest_hbm, tgt_hbm,
    out_ref,
    psi, lenv, renv, src_s, lft_s, rgt_s, dest_s, tgt_s,
    inner, part, core_in, x_out, x_in, a_out, a_in, b_out, b_in, red,
    zslot_out, zslot_in, own, row_out, row_in, slot_out, slot_in, dens, near_out, near_in, far_out, far_in, mid_out, mid_in,
    dcol, tcol, table_s, tables, tables_z, labels, labels_z,
    load_sem, table_sem, table_send, table_recv, table_z_send, table_z_recv,
    core_send, core_recv, x_send, x_recv, a_send, a_recv, b_send, b_recv,
    zs_send, zs_recv, row_send, row_recv, y_send, y_recv, near_send, near_recv, far_send, far_recv, mid_send, mid_recv,
):
    term, sector = lax.axis_index("term"), lax.axis_index("sector")
    x, c = term // NCORE, term % NCORE
    y, z = sector // NZ, sector % NZ
    x_at = [lax.rem(x + d, NX) for d in range(NX)]
    y_at = [lax.rem(y + d, NY) * NZ for d in range(NY)]
    z_at = [lax.rem(z + d, NZ) for d in range(NZ)]

    def at_x(d):
        return (x_at[d] * NCORE + c, sector)

    def at_y(d):
        return (term, y_at[d] + z)

    def at_z(d):
        return (term, y_at[0] + z_at[d])

    partner = (x * NCORE + 1 - c, sector)
    x_dev = (at_x(3), at_x(1))
    z_one = (at_z(7), at_z(1))
    z_two = (at_z(6), at_z(2))

    small = [(src_hbm, src_s), (lft_hbm, lft_s), (rgt_hbm, rgt_s), (dest_hbm, dest_s), (tgt_hbm, tgt_s)]
    loads = small + [(psi_hbm, psi), (right_hbm, renv), (left_hbm, lenv)]
    loads = [pltpu.make_async_copy(a, b, load_sem.at[i]) for i, (a, b) in enumerate(loads)]
    for cp in loads[5:] + loads[:5]:
        cp.start()

    barrier = pltpu.get_barrier_semaphore()
    peers = [partner] + [at_x(d) for d in (1, 2, 3)] + [at_y(d) for d in (1, 2, 3)]
    peers += [at_z(d) for d in range(1, NZ)]
    for dev in peers:
        pl.semaphore_signal(barrier, inc=1, device_id=dev, device_id_type=MESH)

    def remote(src, dst, send, recv, dev):
        return pltpu.make_async_remote_copy(
            src_ref=src, dst_ref=dst, send_sem=send, recv_sem=recv, device_id=dev, device_id_type=MESH
        )

    def arrived(dst, recv):
        remote(dst, dst, recv, recv, partner).wait_recv()

    def left(src, send):
        remote(src, src, send, send, partner).wait_send()

    def compute(b):
        for k in range(TERMS):
            for j in range(BATCH):
                p = b * BATCH + j
                inner[j, k] = jnp.dot(psi[src_s[p]], renv[rgt_s[p], k], preferred_element_type=F32).astype(BF16)
        for j in range(BATCH):
            l = lft_s[b * BATCH + j]
            acc = None
            for k in range(TERMS):
                d = jnp.dot(lenv[l, k], inner[j, k], preferred_element_type=F32)
                acc = d if acc is None else acc + d
            for xx in range(NX):
                for cc in range(NCORE):
                    for h in range(2):
                        r = ((xx * NCORE + cc) * 2 + h) * ROWS
                        part[h, cc, b, xx, j] = acc[r : r + ROWS].astype(BF16)

    def core_copy(h, b):
        return remote(part.at[h, 1 - c, b], core_in.at[h, b], core_send, core_recv.at[h, b], partner)

    def chip_sum(h, b, d, lo=0, hi=BATCH):
        xx = x_at[d]
        return part[h, c, b, xx, lo:hi].astype(F32) + core_in[h, b, xx, lo:hi].astype(F32)

    def x_copy(b, d):
        return remote(x_out.at[b, d - 1], x_in.at[b, d - 1], x_send, x_recv.at[b], at_x(d))

    def stage_x(b):
        arrived(core_in.at[0, b], core_recv.at[0, b])
        for d in (2, 1, 3):
            x_out[b, d - 1] = chip_sum(0, b, d).astype(BF16)
            x_copy(b, d).start()

    def stage_sum0(b):
        arrived(x_in.at[b], x_recv.at[b])
        total = chip_sum(0, b, 0)
        for d in (1, 2, 3):
            total = total + x_in[b, d - 1].astype(F32)
        red[0, pl.ds(b * BATCH, BATCH)] = total.astype(BF16)

    def stage_a(b):
        arrived(core_in.at[1, b], core_recv.at[1, b])
        for d in BOTH:
            a_out[b, d] = chip_sum(1, b, 2, d * SUB, (d + 1) * SUB).astype(BF16)
            remote(a_out.at[b, d], a_in.at[b, d], a_send, a_recv.at[b], x_dev[d]).start()

    def send_b(ch, lo, hi):
        for d in BOTH:
            ps = pl.ds(lo * BATCH, (hi - lo) * BATCH)
            remote(b_out.at[ch, d, ps], b_in.at[ch, d, ps], b_send, b_recv.at[ch], x_dev[d]).start()

    def stage_b(b):
        arrived(a_in.at[b], a_recv.at[b])
        for d in BOTH:
            total = chip_sum(1, b, 3 if d == LEFT else 1)
            extra = a_in[b, d].astype(F32)
            lo, hi = total[:SUB], total[SUB:]
            if d == LEFT:
                lo = lo + extra
            else:
                hi = hi + extra
            total = jnp.concatenate([lo, hi], axis=0).astype(BF16)
            for ch in range(2):
                b_out[ch, d, pl.ds(b * BATCH, BATCH)] = total[:, :, ch * COLS : (ch + 1) * COLS]

    def stage_sum1(ch):
        arrived(b_in.at[ch], b_recv.at[ch])
        cols = slice(ch * COLS, (ch + 1) * COLS)
        for b in range(NB):
            ps = pl.ds(b * BATCH, BATCH)
            xx = x_at[0]
            total = part[1, c, b, xx, :, :, cols].astype(F32) + core_in[1, b, xx, :, :, cols].astype(F32)
            total = total + b_in[ch, LEFT, ps].astype(F32) + b_in[ch, RIGHT, ps].astype(F32)
            red[1, ps, :, cols] = total.astype(BF16)

    def add_slot(acc, blk, lab):
        blk = blk.astype(F32)
        lab = jnp.broadcast_to(lab, (ROWS, COLS))
        for t in range(OWNED):
            term_ = jnp.where(lab == t, blk, 0.0)
            acc[t] = term_ if acc[t] is None else acc[t] + term_

    def send_z(q):
        h, i, cols = q // 2, q, slice((q % 2) * COLS, (q % 2 + 1) * COLS)
        for dz in (4, 3, 5, 2, 6, 1, 7, 0):
            for dy in range(NY):
                o = y_at[dy] + z_at[dz]
                for s in range(CAP):
                    blk = red[h, table_s[s, o], :, cols]
                    if dz:
                        zslot_out[i, dz - 1, dy, s] = blk
                    else:
                        zslot_in[i, 0, dy, s] = blk
            if dz:
                remote(
                    zslot_out.at[i, dz - 1], zslot_in.at[i, dz], zs_send.at[i], zs_recv.at[i], at_z(dz)
                ).start()

    def row_z(q):
        i = q
        arrived(zslot_in.at[i, 1:], zs_recv.at[i])
        for dy in (2, 1, 3, 0):
            acc = [None] * OWNED
            for dz in range(NZ):
                for s in range(CAP):
                    add_slot(acc, zslot_in[i, dz, dy, s], labels_z[dy, dz, 2 + s : 3 + s, :])
            for t in range(OWNED):
                if dy:
                    row_out[i, dy - 1, t] = acc[t].astype(BF16)
                else:
                    own[i, t] = acc[t]
            if dy:
                remote(
                    row_out.at[i, dy - 1], row_in.at[i, dy - 1], row_send.at[i], row_recv.at[i], at_y(dy)
                ).start()

    def finish_z(q):
        h, i, cols = q // 2, q, slice((q % 2) * COLS, (q % 2 + 1) * COLS)
        arrived(row_in.at[i], row_recv.at[i])
        total = own[i]
        for dy in range(1, NY):
            total = total + row_in[i, dy - 1].astype(F32)
        out_ref[:, h * ROWS : (h + 1) * ROWS, cols] = total.astype(BF16)

    def send_y(q):
        h, cols = q // 2, slice((q % 2) * COLS, (q % 2 + 1) * COLS)
        for dy in (2, 1, 3, 0):
            for dz in range(NZ):
                o = y_at[dy] + z_at[dz]
                for s in range(CAP):
                    blk = red[h, table_s[s, o], :, cols]
                    if dy:
                        slot_out[q - 2, dy - 1, dz, s] = blk
                    else:
                        slot_in[q - 2, 0, dz, s] = blk
            if dy:
                remote(slot_out.at[q - 2, dy - 1], slot_in.at[q - 2, dy], y_send, y_recv.at[q - 2], at_y(dy)).start()

    def dense(q, dz):
        acc = [None] * OWNED
        for dy in range(NY):
            for s in range(CAP):
                add_slot(acc, slot_in[q - 2, dy, dz, s], labels[dz, dy, 2 + s : 3 + s, :])
        return acc

    def first_z(q):
        arrived(slot_in.at[q - 2, 1:], y_recv.at[q - 2])
        acc = dense(q, 4)
        for t in range(HALF_T):
            far_out[q - 2, RIGHT, t] = acc[t].astype(BF16)
            far_out[q - 2, LEFT, t] = acc[HALF_T + t].astype(BF16)
        for d in BOTH:
            remote(far_out.at[q - 2, d], far_in.at[q - 2, d], far_send, far_recv.at[q - 2, d], z_two[d]).start()
        for d in BOTH:
            for i, dz in enumerate((1, 3) if d == RIGHT else (7, 5)):
                acc = dense(q, dz)
                for t in range(OWNED):
                    near_out[q - 2, d, i, t] = acc[t].astype(BF16)
            remote(near_out.at[q - 2, d], near_in.at[q - 2, d], near_send, near_recv.at[q - 2, d], z_one[d]).start()
        for i, dz in enumerate((6, 2, 0)):
            acc = dense(q, dz)
            for t in range(OWNED):
                dens[q - 2, i, t] = acc[t]

    def second_z(q):
        for d in BOTH:
            arrived(far_in.at[q - 2, d], far_recv.at[q - 2, d])
            arrived(near_in.at[q - 2, d], near_recv.at[q - 2, d])
            total = dens[q - 2, d] + near_in[q - 2, d, 1].astype(F32)
            far = far_in[q - 2, d].astype(F32)
            lo, hi = total[:HALF_T], total[HALF_T:]
            if d == RIGHT:
                lo = lo + far
            else:
                hi = hi + far
            mid_out[q - 2, d, :HALF_T] = lo.astype(BF16)
            mid_out[q - 2, d, HALF_T:] = hi.astype(BF16)
            remote(mid_out.at[q - 2, d], mid_in.at[q - 2, d], mid_send, mid_recv.at[q - 2, d], z_two[d]).start()

    def finish(q):
        h, cols = q // 2, slice((q % 2) * COLS, (q % 2 + 1) * COLS)
        total = dens[q - 2, 2]
        for d in BOTH:
            total = total + near_in[q - 2, d, 0].astype(F32)
        for d in BOTH:
            arrived(mid_in.at[q - 2, d], mid_recv.at[q - 2, d])
            total = total + mid_in[q - 2, d].astype(F32)
        out_ref[:, h * ROWS : (h + 1) * ROWS, cols] = total.astype(BF16)

    for cp in loads[:5]:
        cp.wait()
    for p in range(PAIRS):
        dcol[p] = jnp.full((128,), dest_s[p], I32)
        tcol[p] = jnp.full((128,), tgt_s[p], I32)
    lane = lax.broadcasted_iota(I32, (PAIRS, 128), 1)
    prow = lax.broadcasted_iota(I32, (PAIRS, 128), 0)
    same = dcol[...] == lane
    low = jnp.min(jnp.where(same, prow, PAIRS), axis=0, keepdims=True)
    high = jnp.max(jnp.where(same, prow, -1), axis=0, keepdims=True)
    low_t = jnp.max(jnp.where(same & (prow == low), tcol[...], -1), axis=0, keepdims=True)
    high_t = jnp.max(jnp.where(same & (prow == high) & (high > low), tcol[...], -1), axis=0, keepdims=True)
    tables[0] = jnp.concatenate(
        [jnp.clip(low, 0, PAIRS - 1), jnp.clip(high, 0, PAIRS - 1), low_t, high_t, jnp.zeros((4, 128), I32)], axis=0
    )
    to_smem = pltpu.make_async_copy(tables.at[0], table_s, table_sem)
    to_smem.start()
    for cp in loads[5:]:
        cp.wait()

    compute(0)
    to_smem.wait()
    pl.semaphore_wait(barrier, len(peers))
    core_copy(0, 0).start()
    core_copy(1, 0).start()
    def send_tables():
        for d in range(1, NY):
            remote(tables.at[0], tables.at[d], table_send, table_recv, at_y(d)).start()
        for d in range(1, NZ):
            remote(tables.at[0], tables_z.at[d], table_z_send, table_z_recv, at_z(d)).start()
        tables_z[0] = tables[0]

    def loop(b, _):
        compute(b)
        core_copy(0, b).start()
        core_copy(1, b).start()
        stage_x(b - 1)
        stage_a(b - 1)

        @pl.when(b == 2)
        def _():
            send_tables()

        return 0

    lax.fori_loop(1, NB, loop, 0)
    stage_x(NB - 1)
    stage_a(NB - 1)
    for b in range(NB - 2):
        stage_b(b)
    send_b(0, 0, NB - 2)
    arrived(tables.at[1:], table_recv)
    arrived(tables_z.at[1:], table_z_recv)
    lane = lax.broadcasted_iota(I32, (NY, 8, 128), 2)
    for dz in range(NZ):
        mine = jnp.sum(jnp.where(lane == y_at[0] + z_at[dz], tables[...], 0), axis=2, keepdims=True)
        labels[dz] = jnp.broadcast_to(mine, (NY, 8, 128))
    lane = lax.broadcasted_iota(I32, (NZ, 8, 128), 2)
    for dy in range(NY):
        mine = jnp.sum(jnp.where(lane == y_at[dy] + z, tables_z[...], 0), axis=2, keepdims=True)
        labels_z[dy] = jnp.broadcast_to(mine, (NZ, 8, 128))
    for b in range(NB):
        stage_sum0(b)
    send_z(0)
    send_z(1)
    for b in range(NB - 2, NB):
        stage_b(b)
    send_b(0, NB - 2, NB)
    send_b(1, 0, NB)
    stage_sum1(0)
    send_y(2)
    stage_sum1(1)
    send_y(3)
    row_z(0)
    first_z(2)
    first_z(3)
    row_z(1)
    second_z(2)
    finish_z(0)
    second_z(3)
    finish_z(1)
    finish(2)
    finish(3)

    left(tables.at[1:], table_send)
    left(tables_z.at[1:], table_z_send)
    left(core_in, core_send)
    left(x_out, x_send)
    left(a_out, a_send)
    left(b_out, b_send)
    for i in range(2):
        left(zslot_out.at[i], zs_send.at[i])
        left(row_out.at[i], row_send.at[i])
    left(slot_out, y_send)
    left(near_out, near_send)
    left(far_out, far_send)
    left(mid_out, mid_send)


def shards(psi, left_env, right_env, pair_source, pair_left, pair_right, pair_dest, pair_target):
    block, tile = (ROWS, WIDTH), (ROWS, COLS)
    dma = pltpu.SemaphoreType.DMA
    return pl.pallas_call(
        kernel,
        out_shape=jax.ShapeDtypeStruct((OWNED, 2 * ROWS, WIDTH), BF16),
        in_specs=[pl.BlockSpec(memory_space=pl.ANY)] * 8,
        out_specs=pl.BlockSpec(memory_space=pltpu.VMEM),
        scratch_shapes=[
            pltpu.VMEM((OWNED, WIDTH, WIDTH), BF16),
            pltpu.VMEM((4, TERMS, WIDTH, WIDTH), BF16),
            pltpu.VMEM((4, TERMS, WIDTH, WIDTH), BF16),
        ]
        + [pltpu.SMEM((PAIRS,), I32)] * 5
        + [
            pltpu.VMEM((BATCH, TERMS, WIDTH, WIDTH), BF16),
            pltpu.VMEM((2, NCORE, NB, NX, BATCH) + block, BF16),
            pltpu.VMEM((2, NB, NX, BATCH) + block, BF16),
            pltpu.VMEM((NB, NX - 1, BATCH) + block, BF16),
            pltpu.VMEM((NB, NX - 1, BATCH) + block, BF16),
            pltpu.VMEM((NB, 2, SUB) + block, BF16),
            pltpu.VMEM((NB, 2, SUB) + block, BF16),
            pltpu.VMEM((2, 2, PAIRS) + tile, BF16),
            pltpu.VMEM((2, 2, PAIRS) + tile, BF16),
            pltpu.VMEM((2, PAIRS) + block, BF16),
            pltpu.VMEM((2, NZ - 1, NY, CAP) + tile, BF16),
            pltpu.VMEM((2, NZ, NY, CAP) + tile, BF16),
            pltpu.VMEM((2, OWNED) + tile, F32),
            pltpu.VMEM((2, NY - 1, OWNED) + tile, BF16),
            pltpu.VMEM((2, NY - 1, OWNED) + tile, BF16),
            pltpu.VMEM((CHUNKS - 2, NY - 1, NZ, CAP) + tile, BF16),
            pltpu.VMEM((CHUNKS - 2, NY, NZ, CAP) + tile, BF16),
            pltpu.VMEM((CHUNKS - 2, 3, OWNED) + tile, F32),
            pltpu.VMEM((CHUNKS - 2, 2, 2, OWNED) + tile, BF16),
            pltpu.VMEM((CHUNKS - 2, 2, 2, OWNED) + tile, BF16),
            pltpu.VMEM((CHUNKS - 2, 2, HALF_T) + tile, BF16),
            pltpu.VMEM((CHUNKS - 2, 2, HALF_T) + tile, BF16),
            pltpu.VMEM((CHUNKS - 2, 2, OWNED) + tile, BF16),
            pltpu.VMEM((CHUNKS - 2, 2, OWNED) + tile, BF16),
            pltpu.VMEM((PAIRS, 128), I32),
            pltpu.VMEM((PAIRS, 128), I32),
            pltpu.SMEM((8, 128), I32),
            pltpu.VMEM((NY, 8, 128), I32),
            pltpu.VMEM((NZ, 8, 128), I32),
            pltpu.VMEM((NZ, NY, 8, 128), I32),
            pltpu.VMEM((NY, NZ, 8, 128), I32),
            dma((8,)), dma, dma, dma, dma, dma,
            dma, dma((2, NB)), dma, dma((NB,)), dma, dma((NB,)), dma, dma((2,)),
            dma((2,)), dma((2,)), dma((2,)), dma((2,)), dma, dma((CHUNKS - 2,)),
            dma, dma((CHUNKS - 2, 2)), dma, dma((CHUNKS - 2, 2)), dma, dma((CHUNKS - 2, 2)),
        ],
        compiler_params=pltpu.CompilerParams(
            collective_id=0, has_side_effects=True, vmem_limit_bytes=56 * 2**20
        ),
        name="sigma",
    )(
        psi,
        left_env.reshape((4, TERMS, WIDTH, WIDTH)),
        right_env.reshape((4, TERMS, WIDTH, WIDTH)),
        pair_source, pair_left, pair_right, pair_dest.reshape(PAIRS), pair_target,
    )


def solution(mesh):
    placed = (
        P("sector", None, None),
        P("term", "sector", None, None, None),
        P("term", "sector", None, None, None),
        P("sector"),
        P("sector"),
        P("sector"),
        P("sector", None),
        P("sector"),
    )
    return jax.shard_map(
        shards, mesh=mesh, in_specs=placed, out_specs=P("sector", "term", None), check_vma=False
    )
```
